32 devices in a mesh: wide: 8 (over z, x), narrow: 4 (over y, core).
Axes of the slice: x: 2, y: 2, z: 4, core: 2. Of those that a mesh axis runs over, the one named last changes fastest.
Arguments:
- rhs: float32 [64, 64, 1024], P(None, 'wide', 'narrow'), may hold values from -6 to 6
- areas: float32 [64, 1024], P('wide', 'narrow'), may hold values from 0.5 to 2
- stiffness: float32 [64], replicated, may hold values from 1e-07 to 1
Outputs:
- pressure: float32 [64, 64, 1024], P(None, 'wide', 'narrow')
- residual: float32 [64, 64, 1024], P(None, 'wide', 'narrow')
The draws below stay inside these ranges and needn't reach their ends.
All inputs are finite; a program needn't handle non-finite values.
Results may differ from the reference program's by a relative error of at most 0.0003.
Values sent between devices are 32-bit elements; how exact they have to be, the bound alone decides.
A program may use at most 64 MiB of HBM per device.

```python
import math
import jax
import jax.numpy as jnp
from jax import lax

K = 64
NX = 64
NY = 1024


def shard_levels(key, shape, split, least, high):
    def one(axis_at, shards_of):
        draws = jax.random.uniform(jax.random.fold_in(jax.random.fold_in(key, 6), axis_at), (shards_of,), jnp.float32, least / len(split), high / len(split))
        return jnp.repeat(jnp.exp(draws), shape[axis_at] // shards_of).reshape((-1,) + (1,) * (len(shape) - axis_at - 1))

    factor_of = one(*split[0])
    for cut in split[1:]:
        factor_of = factor_of * one(*cut)
    return factor_of


def centred(stream_key, shape, deviation, most, shards=(), kind=jnp.bfloat16):
    values = deviation * jax.random.normal(stream_key, shape, jnp.float32)
    if shards:
        values = values * shard_levels(stream_key, shape, shards, -0.22, 0.18)
    return jnp.clip(values, -most, most).astype(kind)


def setup_inputs(seed: int = 0) -> dict:
    seeds = jax.random.split(jax.random.key(seed), 4)
    return {
        "rhs": centred(seeds[0], (K, NX, NY), 1.0, 6.0, ((1, 8), (2, 4)), jnp.float32),
        "areas": jnp.clip(jnp.exp(math.log(2.0) - 1.3862944 * jax.random.uniform(seeds[1], (NX, NY), jnp.float32) ** shard_levels(seeds[1], (NX, NY), ((0, 8), (1, 4)), -0.2, 0.2)), 0.5, 2.0),
        "stiffness": jnp.clip(jnp.exp(jax.random.uniform(seeds[2], (K,), jnp.float32, math.log(1.0000000116860974e-07), math.log(1.0))), 1.0000000116860974e-07, 1.0),
    }


coupling = 2.0
relaxation = 0.4

def column_inverse(stiffness):
    levels = stiffness.shape[0]
    identity_k = jnp.eye(levels, dtype=stiffness.dtype)
    neighbours = jnp.eye(levels, k=1, dtype=stiffness.dtype) + jnp.eye(levels, k=-1, dtype=stiffness.dtype)
    matrix = jnp.diag(stiffness + 2.0 * coupling + 4.0) - coupling * neighbours
    lower = jnp.linalg.cholesky(matrix)
    lower_inv = lax.linalg.triangular_solve(lower, identity_k, left_side=True, lower=True)
    return jnp.dot(lower_inv.T, lower_inv, precision=lax.Precision.HIGHEST)

def apply_columns(inverse, field):
    return jnp.einsum('kl,lxy->kxy', inverse, field, precision=lax.Precision.HIGHEST)

def vertical(field, stiffness):
    empty = jnp.zeros_like(field[:1])
    above = jnp.concatenate([field[1:], empty], axis=0)
    below = jnp.concatenate([empty, field[:-1]], axis=0)
    return stiffness[:, None, None] * field + coupling * (2.0 * field - above - below)

def operate(padded, coef, stiffness):
    center = padded[:, 1:-1, 1:-1]
    beside = padded[:, 2:, 1:-1] + padded[:, :-2, 1:-1] + padded[:, 1:-1, 2:] + padded[:, 1:-1, :-2]
    return vertical(center, stiffness) + coef[None] * (4.0 * center - beside)

def coarsen(field):
    return 0.25 * (field[..., 0::2, 0::2] + field[..., 1::2, 0::2] + field[..., 0::2, 1::2] + field[..., 1::2, 1::2])

def line_factors(stiffness):
    gain_in = jnp.sqrt(stiffness + 0.25 * stiffness * stiffness) - 0.5 * stiffness
    return (gain_in, 1.0 - gain_in)

def pad_zero(field):
    return jnp.pad(field, ((0, 0), (1, 1), (1, 1)))

def reference(rhs, areas, stiffness):
    inverse = column_inverse(stiffness)

    def residual_of(field):
        return rhs - operate(pad_zero(field), areas, stiffness)
    field = relaxation * apply_columns(inverse, rhs)
    field = field + relaxation * apply_columns(inverse, residual_of(field))
    coarse_rhs = coarsen(residual_of(field))
    coarse_coef = 0.25 * coarsen(areas)
    gain_in, retain = line_factors(stiffness)

    def advance(carry, column):
        fresh = gain_in[:, None] * column + retain[:, None] * carry
        return (fresh, fresh)
    columns = jnp.moveaxis(coarse_rhs, 1, 0)
    empty = jnp.zeros_like(columns[0])
    _, forward = lax.scan(advance, empty, columns)
    _, backward = lax.scan(advance, empty, forward, reverse=True)
    line_corr = jnp.moveaxis(backward, 0, 1)
    coarse_corr = line_corr + relaxation * apply_columns(inverse, coarse_rhs - operate(pad_zero(line_corr), coarse_coef, stiffness))
    field = field + jnp.repeat(jnp.repeat(coarse_corr, 2, axis=1), 2, axis=2)
    field = field + relaxation * apply_columns(inverse, residual_of(field))
    field = field + relaxation * apply_columns(inverse, residual_of(field))
    return (field, residual_of(field))
```

```python
import functools

import jax
import jax.numpy as jnp
from jax import lax
from jax.experimental import pallas as pl
from jax.experimental.pallas import tpu as pltpu
from jax.sharding import PartitionSpec as P

MESH = pl.DeviceIdType.MESH
f32 = jnp.float32
bf16 = jnp.bfloat16


def halves(value):
    high = value.astype(bf16)
    return high, (value - high.astype(f32)).astype(bf16)


def kernel(
    n_w, n_n, nx, ny, levels,
    rhs_ref, areas_ref, stiff_ref, p_out, r_out,
    fields, rhs_x, halo_x, pack_y, halo_y,
    line, line_hx, line_py, line_hy, scan_f, scan_z, scan_rf, scan_rz, theta, phi, stiff_b,
    send_sem, recv_sem, scan_send, scan_recv,
):
    cx, cy = nx // 2, ny // 2
    w, c = lax.axis_index("wide"), lax.axis_index("narrow")
    has = (w > 0, w < n_w - 1, c > 0, c < n_n - 1)
    to = (
        {"wide": jnp.maximum(w - 1, 0)},
        {"wide": jnp.minimum(w + 1, n_w - 1)},
        {"narrow": jnp.maximum(c - 1, 0)},
        {"narrow": jnp.minimum(c + 1, n_n - 1)},
    )
    strides = []
    while (1 << len(strides)) < n_w:
        strides.append(1 << len(strides))

    nothing = jnp.zeros((levels, ny), f32)
    small = nothing[:, :128]
    for side in range(2):
        @pl.when(jnp.logical_not(has[side]))
        def _():
            for stage in range(5):
                halo_x[stage, side] = nothing
            line_hx[side] = small

        @pl.when(jnp.logical_not(has[2 + side]))
        def _():
            for stage in range(5):
                halo_y[stage, side] = small
            line_hy[side] = small
    for i, s in enumerate(strides):
        @pl.when(w < s)
        def _():
            scan_rf[i] = small

        @pl.when(w >= n_w - s)
        def _():
            scan_rz[i] = small

    barrier = pltpu.get_barrier_semaphore()
    for side in range(4):
        @pl.when(has[side])
        def _():
            pl.semaphore_signal(barrier, inc=1, device_id=to[side], device_id_type=MESH)
    for s in strides[1:]:
        @pl.when(w >= s)
        def _():
            pl.semaphore_signal(
                barrier, inc=1, device_id={"wide": jnp.maximum(w - s, 0)}, device_id_type=MESH
            )

        @pl.when(w < n_w - s)
        def _():
            pl.semaphore_signal(
                barrier, inc=1, device_id={"wide": jnp.minimum(w + s, n_w - 1)}, device_id_type=MESH
            )

    before, now = jnp.float32(0.0), jnp.float32(1.0)
    for i in range(levels):
        theta[i : i + 1, :] = jnp.full((1, 128), now, f32)
        before, now = now, (stiff_ref[i] * 0.125 + 1.0) * now - 0.0625 * before
        stiff_b[i : i + 1, :] = jnp.full((1, 128), stiff_ref[i], f32)
    whole = jnp.full((levels, 128), now, f32)
    before, now = jnp.float32(0.0), jnp.float32(1.0)
    for i in reversed(range(levels)):
        phi[i : i + 1, :] = jnp.full((1, 128), now, f32)
        before, now = now, (stiff_ref[i] * 0.125 + 1.0) * now - 0.0625 * before
    row = lax.broadcasted_iota(jnp.int32, (levels, 128), 0)
    col = lax.broadcasted_iota(jnp.int32, (levels, 128), 1)
    apart = jnp.abs(row - col)
    decay = jnp.full((levels, 128), 0.4 * 0.125, f32)
    for b in range(6):
        decay = jnp.where((apart & (1 << b)) != 0, decay * (0.25 ** (1 << b)), decay)
    t_col, p_col = theta[...], phi[...]
    same = row == col
    t_row = jnp.sum(jnp.where(same, t_col, 0.0), axis=0, keepdims=True)
    p_row = jnp.sum(jnp.where(same, p_col, 0.0), axis=0, keepdims=True)
    inverse = (jnp.where(row <= col, t_col * p_row, p_col * t_row) * decay / whole)[:, :levels]
    inv_hi, inv_lo = halves(inverse)
    weights = jnp.concatenate([inv_hi, inv_hi, inv_lo], axis=1)

    def apply(value):
        high, low = halves(value)
        stacked = jnp.concatenate([high, low, high], axis=0)
        return jnp.dot(weights, stacked, preferred_element_type=f32)

    lane = lax.broadcasted_iota(jnp.int32, (levels, ny), 1)
    lane_c = lax.broadcasted_iota(jnp.int32, (levels, 128), 1)
    level = lax.broadcasted_iota(jnp.int32, (levels, ny), 0)

    def copies(stage):
        if stage < 5:
            sources = (fields.at[stage, 0], fields.at[stage, nx - 1], pack_y.at[stage, 0], pack_y.at[stage, 1])
            targets = (halo_x.at[stage, 1], halo_x.at[stage, 0], halo_y.at[stage, 1], halo_y.at[stage, 0])
        else:
            sources = (line.at[0], line.at[cx - 1], line_py.at[0], line_py.at[1])
            targets = (line_hx.at[1], line_hx.at[0], line_hy.at[1], line_hy.at[0])
        return [
            pltpu.make_async_remote_copy(
                src_ref=sources[i], dst_ref=targets[i], send_sem=send_sem.at[stage, i],
                recv_sem=recv_sem.at[stage, i], device_id=to[i], device_id_type=MESH,
            )
            for i in range(4)
        ]

    def start(stage, sides):
        every = copies(stage)
        for i in sides:
            @pl.when(has[i])
            def _():
                every[i].start()

    def arrive(stage):
        every = copies(stage)
        for i in range(4):
            @pl.when(has[i ^ 1])
            def _():
                every[i].wait_recv()

    def sent(stage):
        every = copies(stage)
        for i in range(4):
            @pl.when(has[i])
            def _():
                every[i].wait_send()

    order = (0, nx - 1) + tuple(range(1, nx - 1))

    def run(stage, compute):
        first = jnp.zeros((levels, 128), f32)
        last = jnp.zeros((levels, 128), f32)
        for at, x in enumerate(order):
            new = compute(x)
            fields[stage, x] = new
            if at == 1:
                start(stage, (0, 1))
            first = jnp.where(lane_c == x, pltpu.roll(new[:, :128], x, 1) if x else new[:, :128], first)
            last = jnp.where(lane_c == x, pltpu.roll(new[:, ny - 128 :], x + 1, 1), last)
        pack_y[stage, 0] = first
        pack_y[stage, 1] = last
        start(stage, (2, 3))

    def beside(stage, x):
        u = fields[stage, x]
        left = fields[stage, x - 1] if x else halo_x[stage, 0]
        right = fields[stage, x + 1] if x < nx - 1 else halo_x[stage, 1]
        low = halo_y[stage, 0]
        low = pltpu.roll(low, 128 - x, 1) if x else low
        high = pltpu.roll(halo_y[stage, 1], 127 - x, 1)
        edge = jnp.concatenate([low, high], axis=1)
        down = jnp.where(lane == 0, edge, pltpu.roll(u, 1, 1))
        up = jnp.where(lane == ny - 1, edge, pltpu.roll(u, ny - 1, 1))
        return u, left + right + down + up

    def smooth(stage, x):
        u, nb = beside(stage, x)
        a = areas_ref[x : x + 1, :]
        return 0.6 * u + apply(rhs_x[x] + (4.0 - 4.0 * a) * u + a * nb)

    def horizontal(stage, x):
        u, nb = beside(stage, x)
        a = areas_ref[x : x + 1, :]
        return u, rhs_x[x] - a * (4.0 * u - nb)

    def vertical(v):
        above = jnp.where(level == levels - 1, 0.0, pltpu.roll(v, levels - 1, 0))
        below = jnp.where(level == 0, 0.0, pltpu.roll(v, 1, 0))
        s = jnp.concatenate([stiff_b[...]] * (ny // 128), axis=1)
        return (s + 4.0) * v - 2.0 * (above + below)

    for x in range(nx):
        rhs_x[x] = rhs_ref[:, x, :]

    peers = sum(h.astype(jnp.int32) for h in has)
    for s in strides[1:]:
        peers = peers + (w >= s).astype(jnp.int32) + (w < n_w - s).astype(jnp.int32)
    pl.semaphore_wait(barrier, peers)

    run(0, lambda x: apply(rhs_x[x]))
    arrive(0)
    run(1, lambda x: smooth(0, x))

    s = stiff_b[...]
    keep = jnp.sqrt(s + 0.25 * s * s) - 0.5 * s
    r = 1.0 - keep
    power = [jnp.ones_like(r)]
    for _ in range(2 * cx + 1):
        power.append(power[-1] * r)
    tail = jnp.ones_like(r)
    base = power[2 * cx]
    for b in range(len(strides)):
        tail = jnp.where(((n_w - 1 - w) >> b) % 2 == 1, tail * base, tail)
        base = base * base
    scale = keep / (1.0 + r)
    pick = jnp.where(
        lax.broadcasted_iota(jnp.int32, (ny, cy), 0) // 2 == lax.broadcasted_iota(jnp.int32, (ny, cy), 1),
        1.0, 0.0,
    ).astype(bf16)
    spread = jnp.where(
        lax.broadcasted_iota(jnp.int32, (cy, ny), 1) // 2 == lax.broadcasted_iota(jnp.int32, (cy, ny), 0),
        1.0, 0.0,
    ).astype(bf16)

    def coarsen(pairs):
        rows = pairs.shape[0]
        high, low = halves(pairs)
        both = jnp.dot(jnp.concatenate([high, low], axis=0), pick, preferred_element_type=f32)
        return both[:rows] + both[rows:]

    pad_coef = [areas_ref[2 * x : 2 * x + 1, :] + areas_ref[2 * x + 1 : 2 * x + 2, :] for x in range(cx)]
    coef = [coarsen(jnp.broadcast_to(0.0625 * v, (16, ny)))[:1] for v in pad_coef]

    arrive(1)
    coarse = []
    for x in range(cx):
        u_a, h_a = horizontal(1, 2 * x)
        u_b, h_b = horizontal(1, 2 * x + 1)
        coarse.append(coarsen(0.25 * (h_a + h_b - vertical(u_a + u_b))))

    forward = coarse[0]
    for x in range(1, cx):
        forward = coarse[x] + r * forward
    backward = sum((power[x] - tail * power[2 * cx - x]) * coarse[x] for x in range(cx))
    enter = jnp.zeros_like(forward)
    leave = jnp.zeros_like(forward)
    step_all = power[cx]
    step_less = None
    for i, s in enumerate(strides):
        scan_f[i] = forward
        scan_z[i] = backward
        right = pltpu.make_async_remote_copy(
            src_ref=scan_f.at[i], dst_ref=scan_rf.at[i], send_sem=scan_send.at[i, 0], recv_sem=scan_recv.at[i, 0],
            device_id={"wide": jnp.minimum(w + s, n_w - 1)}, device_id_type=MESH,
        )
        left = pltpu.make_async_remote_copy(
            src_ref=scan_z.at[i], dst_ref=scan_rz.at[i], send_sem=scan_send.at[i, 1], recv_sem=scan_recv.at[i, 1],
            device_id={"wide": jnp.maximum(w - s, 0)}, device_id_type=MESH,
        )

        @pl.when(w < n_w - s)
        def _():
            right.start()

        @pl.when(w >= s)
        def _():
            left.start()

        @pl.when(w >= s)
        def _():
            right.wait_recv()

        @pl.when(w < n_w - s)
        def _():
            left.wait_recv()

        got_f, got_z = scan_rf[i], scan_rz[i]
        enter = enter + (got_f if step_less is None else step_less * got_f)
        leave = leave + (got_z if step_less is None else step_less * got_z)
        forward = forward + step_all * got_f
        backward = backward + step_all * got_z
        step_less = power[cx] if step_less is None else step_less * step_all
        step_all = step_all * step_all

        @pl.when(w < n_w - s)
        def _():
            right.wait_send()

        @pl.when(w >= s)
        def _():
            left.wait_send()

    first = jnp.zeros((levels, 128), f32)
    last = jnp.zeros((levels, 128), f32)
    for x in range(cx):
        total = (power[x + 1] - tail * power[2 * cx + 1 - x]) * enter + power[cx - x] * leave
        for j in range(cx):
            total = total + (power[abs(x - j)] - tail * power[2 * cx - x - j]) * coarse[j]
        total = scale * total
        line[x] = total
        first = jnp.where(lane_c == x, pltpu.roll(total, x, 1) if x else total, first)
        last = jnp.where(lane_c == x, pltpu.roll(total, x + 1, 1), last)
    line_py[0] = first
    line_py[1] = last
    start(5, range(4))
    arrive(5)

    def correction(x):
        v = line[x]
        left = line[x - 1] if x else line_hx[0]
        right = line[x + 1] if x < cx - 1 else line_hx[1]
        low = pltpu.roll(line_hy[0], 128 - x, 1) if x else line_hy[0]
        high = pltpu.roll(line_hy[1], 127 - x, 1)
        down = jnp.where(lane_c == 0, low, pltpu.roll(v, 1, 1))
        up = jnp.where(lane_c == cy - 1, high, pltpu.roll(v, cy - 1, 1))
        a = coef[x]
        value = 0.6 * v + apply(coarse[x] + (4.0 - 4.0 * a) * v + a * (left + right + down + up))
        high, low = halves(value)
        both = jnp.dot(jnp.concatenate([high, low], axis=0), spread, preferred_element_type=f32)
        return both[:levels] + both[levels:]

    corrections = {}

    def corrected(x):
        if x // 2 not in corrections:
            corrections[x // 2] = correction(x // 2)
        return fields[1, x] + corrections[x // 2]

    run(2, corrected)
    arrive(2)
    run(3, lambda x: smooth(2, x))
    arrive(3)
    run(4, lambda x: smooth(3, x))
    for x in range(nx):
        p_out[:, x, :] = fields[4, x]
    arrive(4)
    for x in range(nx):
        u, h = horizontal(4, x)
        r_out[:, x, :] = h - vertical(u)
    for stage in range(6):
        sent(stage)


def local(n_w, n_n, rhs, areas, stiffness):
    levels, nx, ny = rhs.shape
    cx = nx // 2
    steps = max(1, (n_w - 1).bit_length())
    vmem = lambda *shape: pltpu.VMEM(shape, f32)
    whole = pl.BlockSpec(memory_space=pltpu.VMEM)
    return pl.pallas_call(
        functools.partial(kernel, n_w, n_n, nx, ny, levels),
        out_shape=[jax.ShapeDtypeStruct(rhs.shape, f32)] * 2,
        in_specs=[whole, whole, pl.BlockSpec(memory_space=pltpu.SMEM)],
        out_specs=[whole, whole],
        scratch_shapes=[
            vmem(5, nx, levels, ny), vmem(nx, levels, ny), vmem(5, 2, levels, ny),
            vmem(5, 2, levels, 128), vmem(5, 2, levels, 128),
            vmem(cx, levels, 128), vmem(2, levels, 128), vmem(2, levels, 128), vmem(2, levels, 128),
            vmem(steps, levels, 128), vmem(steps, levels, 128),
            vmem(steps, levels, 128), vmem(steps, levels, 128),
            vmem(levels, 128), vmem(levels, 128), vmem(levels, 128),
            pltpu.SemaphoreType.DMA((6, 4)), pltpu.SemaphoreType.DMA((6, 4)),
            pltpu.SemaphoreType.DMA((steps, 2)), pltpu.SemaphoreType.DMA((steps, 2)),
        ],
        compiler_params=pltpu.CompilerParams(
            collective_id=0, has_side_effects=True, vmem_limit_bytes=40 * 1024 * 1024
        ),
        cost_estimate=pl.CostEstimate(flops=80_000_000, bytes_accessed=1_600_000, transcendentals=0),
    )(rhs, areas, stiffness)


def solution(mesh):
    placed = (P(None, "wide", "narrow"), P("wide", "narrow"), P())
    return jax.shard_map(
        functools.partial(local, mesh.shape["wide"], mesh.shape["narrow"]),
        mesh=mesh,
        in_specs=placed,
        out_specs=(P(None, "wide", "narrow"), P(None, "wide", "narrow")),
        check_vma=False,
    )
```

```python
import functools

import jax
import jax.numpy as jnp
from jax import lax
from jax.experimental import pallas as pl
from jax.experimental.pallas import tpu as pltpu
from jax.sharding import PartitionSpec as P

MESH = pl.DeviceIdType.MESH
f32 = jnp.float32
bf16 = jnp.bfloat16


def halves(value):
    high = value.astype(bf16)
    return high, (value - high.astype(f32)).astype(bf16)


def kernel(
    n_w, n_n, nx, ny, levels,
    rhs_ref, areas_ref, stiff_ref, p_out, r_out,
    rhs_x, u1, u2, u3, u4, p, wide_a, coarse, line, pack, strip, corner, pack_a, strip_a,
    scan_f, scan_z, scan_rf, scan_rz, theta, phi, stiff_b,
    send_sem, recv_sem, scan_send, scan_recv,
):
    cx, cy = nx // 2, ny // 2
    w, c = lax.axis_index("wide"), lax.axis_index("narrow")
    has = (w > 0, w < n_w - 1, c > 0, c < n_n - 1)
    to = (
        {"wide": jnp.maximum(w - 1, 0)},
        {"wide": jnp.minimum(w + 1, n_w - 1)},
        {"narrow": jnp.maximum(c - 1, 0)},
        {"narrow": jnp.minimum(c + 1, n_n - 1)},
    )
    strides = []
    while (1 << len(strides)) < n_w:
        strides.append(1 << len(strides))
    own = 3

    small = jnp.zeros((levels, 128), f32)
    nothing = jnp.zeros((levels, ny), f32)
    edge_x = (
        ((1, 2), (0, 1), (0, 1, 2, 3)),
        ((nx + 3, nx + 4), (nx + 4, nx + 5), (cx + 4, cx + 5, cx + 6, cx + 7)),
    )
    rhs_x[0] = nothing
    rhs_x[nx + 5] = nothing
    for side in range(2):
        @pl.when(jnp.logical_not(has[side]))
        def _():
            for e in edge_x[side][0]:
                rhs_x[e] = nothing
            for e in edge_x[side][1]:
                u2[e] = nothing
            for e in edge_x[side][2]:
                coarse[e] = small
            corner[0, side] = small
            corner[1, side] = small
            wide_a[2 * side * nx : 2 * side * nx + nx, :] = jnp.zeros((nx, ny), f32)

        @pl.when(jnp.logical_not(has[2 + side]))
        def _():
            strip[side] = small
            strip[2 + 2 * side] = small
            strip[3 + 2 * side] = small
            strip_a[side] = jnp.zeros((16, 128), f32)
    for i, s in enumerate(strides):
        @pl.when(w < s)
        def _():
            scan_rf[i] = small

        @pl.when(w >= n_w - s)
        def _():
            scan_rz[i] = small

    barrier = pltpu.get_barrier_semaphore()
    for side in range(4):
        @pl.when(has[side])
        def _():
            pl.semaphore_signal(barrier, inc=1, device_id=to[side], device_id_type=MESH)
    for s in strides[1:]:
        @pl.when(w >= s)
        def _():
            pl.semaphore_signal(
                barrier, inc=1, device_id={"wide": jnp.maximum(w - s, 0)}, device_id_type=MESH
            )

        @pl.when(w < n_w - s)
        def _():
            pl.semaphore_signal(
                barrier, inc=1, device_id={"wide": jnp.minimum(w + s, n_w - 1)}, device_id_type=MESH
            )

    exchanges = {
        "areas": (0, (wide_a.at[pl.ds(nx, nx)], wide_a.at[pl.ds(2 * nx, nx)]),
                  (wide_a.at[pl.ds(nx, nx)], wide_a.at[pl.ds(0, nx)])),
        "rhs": (0, (rhs_x.at[pl.ds(own, 2)], rhs_x.at[pl.ds(own + nx, 2)]),
                (rhs_x.at[pl.ds(own + nx - 2, 2)], rhs_x.at[pl.ds(own - 2, 2)])),
        "corner": (0, (pack.at[1], corner.at[0, 1]), (pack.at[1], corner.at[0, 0])),
        "u2": (0, (u2.at[pl.ds(own + 1, 2)], u2.at[pl.ds(own + nx + 1, 2)]),
               (u2.at[pl.ds(own + nx - 3, 2)], u2.at[pl.ds(own - 3, 2)])),
        "u2corner": (0, (pack.at[2], corner.at[1, 1]), (pack.at[2], corner.at[1, 0])),
        "coarse": (0, (coarse.at[pl.ds(4, cx)], coarse.at[pl.ds(4 + cx, cx)]),
                   (coarse.at[pl.ds(4, cx)], coarse.at[pl.ds(4 - cx, cx)])),
        "strip": (1, (pack.at[0], strip.at[1]), (pack.at[0], strip.at[0])),
        "strip_a": (1, (pack_a, strip_a.at[1]), (pack_a, strip_a.at[0])),
        "line": (1, (pack.at[pl.ds(3, 2)], strip.at[pl.ds(4, 2)]), (pack.at[pl.ds(3, 2)], strip.at[pl.ds(2, 2)])),
    }
    names = list(exchanges)

    def copies(name):
        axis, low, high = exchanges[name]
        at = names.index(name)
        return [
            (
                pltpu.make_async_remote_copy(
                    src_ref=pair[0], dst_ref=pair[1], send_sem=send_sem.at[at, i], recv_sem=recv_sem.at[at, i],
                    device_id=to[2 * axis + i], device_id_type=MESH,
                ),
                has[2 * axis + i],
                has[2 * axis + 1 - i],
            )
            for i, pair in enumerate((low, high))
        ]

    def start(name):
        for copy, goes, _ in copies(name):
            @pl.when(goes)
            def _():
                copy.start()

    def arrive(*which):
        for name in which:
            for copy, _, comes in copies(name):
                @pl.when(comes)
                def _():
                    copy.wait_recv()

    lane = lax.broadcasted_iota(jnp.int32, (levels, ny), 1)
    lane_c = lax.broadcasted_iota(jnp.int32, (levels, 128), 1)
    level = lax.broadcasted_iota(jnp.int32, (levels, ny), 0)
    inner = lane_c % 8 < 4
    row_c = lane_c // 8

    def packed(rows, base=None):
        result = jnp.zeros((levels, 128), f32) if base is None else base
        for e, value in rows:
            ends = jnp.where(lane_c < 4, value[:, :128], value[:, value.shape[1] - 128 :])
            result = jnp.where(row_c == e, pltpu.roll(ends, 8 * e + 4, 1), result)
        return result

    def strips(mine, low, high):
        return jnp.concatenate([jnp.where(inner, low, mine), jnp.where(inner, mine, high)], axis=1)

    wide_a[nx : 2 * nx, :] = areas_ref[...]
    for x in (0, 1, nx - 2, nx - 1) + tuple(range(2, nx - 2)):
        rhs_x[own + x] = rhs_ref[:, x, :]
    peers = sum(h.astype(jnp.int32) for h in has)
    for s in strides[1:]:
        peers = peers + (w >= s).astype(jnp.int32) + (w < n_w - s).astype(jnp.int32)
    pl.semaphore_wait(barrier, peers)
    start("areas")
    start("rhs")
    pack_rhs = packed([(e, rhs_x[e]) for e in range(own, own + nx)])
    pack[0] = pack_rhs
    start("strip")

    before, now = jnp.float32(0.0), jnp.float32(1.0)
    for i in range(levels):
        theta[i : i + 1, :] = jnp.full((1, 128), now, f32)
        before, now = now, (stiff_ref[i] * 0.125 + 1.0) * now - 0.0625 * before
        stiff_b[i : i + 1, :] = jnp.full((1, 128), stiff_ref[i], f32)
    whole = jnp.full((levels, 128), now, f32)
    before, now = jnp.float32(0.0), jnp.float32(1.0)
    for i in reversed(range(levels)):
        phi[i : i + 1, :] = jnp.full((1, 128), now, f32)
        before, now = now, (stiff_ref[i] * 0.125 + 1.0) * now - 0.0625 * before
    row = lax.broadcasted_iota(jnp.int32, (levels, 128), 0)
    col = lax.broadcasted_iota(jnp.int32, (levels, 128), 1)
    apart = jnp.abs(row - col)
    decay = jnp.full((levels, 128), 0.4 * 0.125, f32)
    for b in range(6):
        decay = jnp.where((apart & (1 << b)) != 0, decay * (0.25 ** (1 << b)), decay)
    t_col, p_col = theta[...], phi[...]
    same = row == col
    t_row = jnp.sum(jnp.where(same, t_col, 0.0), axis=0, keepdims=True)
    p_row = jnp.sum(jnp.where(same, p_col, 0.0), axis=0, keepdims=True)
    inverse = (jnp.where(row <= col, t_col * p_row, p_col * t_row) * decay / whole)[:, :levels]
    inv_hi, inv_lo = halves(inverse)
    weights = jnp.concatenate([inv_hi, inv_hi, inv_lo], axis=1)

    def apply(value):
        high, low = halves(value)
        stacked = jnp.concatenate([high, low, high], axis=0)
        return jnp.dot(weights, stacked, preferred_element_type=f32)

    def area(e):
        return wide_a[nx + e - own : nx + e - own + 1, :]

    def sides(u, sides_of, e):
        n = u.shape[1]
        index = lane[:, :n]
        low = pltpu.roll(sides_of[:, :128], (125 - 8 * e) % 128, 1)
        high = pltpu.roll(sides_of[:, 128:], (123 - 8 * e) % 128, 1)
        if n == 128:
            down = jnp.where(index == 0, low, pltpu.roll(u, 1, 1))
            return down + jnp.where(index == n - 1, high, pltpu.roll(u, n - 1, 1))
        edge = jnp.concatenate([low, high], axis=1)
        down = jnp.where(index == 0, edge, pltpu.roll(u, 1, 1))
        return down + jnp.where(index == n - 1, edge, pltpu.roll(u, n - 1, 1))

    def smooth(field, sides_of, e):
        u = field[e]
        nb = field[e - 1] + field[e + 1] + sides(u, sides_of, e)
        a = area(e)
        return 0.6 * u + apply(rhs_x[e] + (4.0 - 4.0 * a) * u + a * nb)

    def smooth_strip(s, right_side, a):
        nb = pltpu.roll(s, 1, 1) + pltpu.roll(s, ny - 1, 1) + pltpu.roll(s, 8, 1) + pltpu.roll(s, ny - 8, 1)
        return 0.6 * s + apply(right_side + (4.0 - 4.0 * a) * s + a * nb)

    def horizontal(field, sides_of, e):
        u = field[e]
        nb = field[e - 1] + field[e + 1] + sides(u, sides_of, e)
        return u, rhs_x[e] - area(e) * (4.0 * u - nb)

    def vertical(v):
        above = jnp.where(level == levels - 1, 0.0, pltpu.roll(v, levels - 1, 0))
        below = jnp.where(level == 0, 0.0, pltpu.roll(v, 1, 0))
        s = jnp.concatenate([stiff_b[...]] * (ny // 128), axis=1)
        return (s + 4.0) * v - 2.0 * (above + below)

    pick = jnp.where(
        lax.broadcasted_iota(jnp.int32, (ny, cy), 0) // 2 == lax.broadcasted_iota(jnp.int32, (ny, cy), 1),
        1.0, 0.0,
    ).astype(bf16)
    spread = jnp.where(
        lax.broadcasted_iota(jnp.int32, (cy, ny), 1) // 2 == lax.broadcasted_iota(jnp.int32, (cy, ny), 0),
        1.0, 0.0,
    ).astype(bf16)
    fine_lane = lax.broadcasted_iota(jnp.int32, (128, 128), 1)
    spread_strip = jnp.where(
        lax.broadcasted_iota(jnp.int32, (128, 128), 0)
        == 8 * ((fine_lane // 8 + 3) // 2) + 2 + (fine_lane % 8) // 2,
        1.0, 0.0,
    ).astype(bf16)

    def exact(value, matrix):
        rows = value.shape[0]
        high, low = halves(value)
        both = jnp.dot(jnp.concatenate([high, low], axis=0), matrix, preferred_element_type=f32)
        return both[:rows] + both[rows:]

    for e in range(own, own + nx):
        u1[e] = apply(rhs_x[e])

    arrive("strip")
    halo = jnp.where(inner, strip[0], strip[1])
    pack[1] = halo
    start("corner")
    first = apply(strips(pack_rhs, halo, halo))
    for e in range(own + 1, own + nx - 1):
        u2[e] = smooth(u1, first, e)

    arrive("areas")
    eight = lane_c[:8]
    packed_a = jnp.zeros((8, 128), f32)
    for e in range(0, nx + 6):
        v = jnp.broadcast_to(area(e), (8, ny))
        v = pltpu.roll(jnp.where(eight < 4, v[:, :128], v[:, ny - 128 :]), 8 * e + 4, 1)
        packed_a = jnp.where(eight // 8 == e, v, packed_a)
    sums = []
    for x in range(-2, cx + 2):
        at = nx + 2 * x
        sums.append(jnp.broadcast_to(0.0625 * (wide_a[at : at + 1, :] + wide_a[at + 1 : at + 2, :]), (8, ny)))
    coef = exact(jnp.concatenate(sums, axis=0), pick)
    coef = {x: coef[8 * (x + 2) : 8 * (x + 2) + 8] for x in range(-2, cx + 2)}
    packed_c = jnp.zeros((8, 128), f32)
    for x in range(-2, cx + 2):
        v = pltpu.roll(coef[x], 8 * (x + 3) + 4, 1)
        packed_c = jnp.where(eight // 8 == x + 3, v, packed_c)
    pack_a[0:8, :] = packed_a
    pack_a[8:16, :] = packed_c
    start("strip_a")

    arrive("rhs")
    outer = (own - 2, own - 1, own + nx, own + nx + 1)
    for e in outer:
        u1[e] = apply(rhs_x[e])
    pack_all = packed([(e, rhs_x[e]) for e in outer], pack_rhs)
    arrive("corner", "strip_a")
    halo = jnp.where(
        row_c < own, pltpu.roll(corner[0, 0], 64, 1),
        jnp.where(row_c >= own + nx, pltpu.roll(corner[0, 1], 64, 1), halo),
    )
    rhs_strip = strips(pack_all, halo, halo)
    inner_a = eight % 8 < 4

    def strips_a(low, high, mine):
        return jnp.concatenate([jnp.where(inner_a, low, mine), jnp.where(inner_a, mine, high)], axis=1)[:1]

    a_strip = strips_a(strip_a[0, 0:8, :], strip_a[1, 0:8, :], packed_a)
    c_strip = strips_a(strip_a[0, 8:16, :], strip_a[1, 8:16, :], packed_c)
    first = apply(rhs_strip)
    for e in (own - 1, own, own + nx - 1, own + nx):
        u2[e] = smooth(u1, first, e)
    second = smooth_strip(first, rhs_strip, a_strip)

    s = stiff_b[...]
    keep = jnp.sqrt(s + 0.25 * s * s) - 0.5 * s
    r = 1.0 - keep
    power = [jnp.ones_like(r)]
    for _ in range(4 * cx):
        power.append(power[-1] * r)
    is_last = w == n_w - 1
    far = jnp.ones_like(r)
    base = power[2 * cx]
    steps = jnp.maximum(n_w - 2 - w, 0)
    for b in range(len(strides)):
        far = jnp.where((steps >> b) % 2 == 1, far * base, far)
        base = base * base
    tail = jnp.where(is_last, power[0], far * power[2 * cx])
    scale = keep / (1.0 + r)

    for x in range(cx):
        e = own + 2 * x
        u_a, h_a = horizontal(u2, second, e)
        u_b, h_b = horizontal(u2, second, e + 1)
        coarse[4 + x] = exact(0.25 * (h_a + h_b - vertical(u_a + u_b)), pick)
    mine = [coarse[4 + x] for x in range(cx)]
    forward = mine[0]
    for x in range(1, cx):
        forward = mine[x] + r * forward
    backward = sum((power[x] - tail * power[2 * cx - x]) * mine[x] for x in range(cx))
    enter = jnp.zeros_like(forward)
    leave = jnp.zeros_like(forward)
    step_all = power[cx]
    step_less = None
    scans = []
    for i, s in enumerate(strides):
        scan_f[i] = forward
        scan_z[i] = backward
        right = pltpu.make_async_remote_copy(
            src_ref=scan_f.at[i], dst_ref=scan_rf.at[i], send_sem=scan_send.at[i, 0], recv_sem=scan_recv.at[i, 0],
            device_id={"wide": jnp.minimum(w + s, n_w - 1)}, device_id_type=MESH,
        )
        left = pltpu.make_async_remote_copy(
            src_ref=scan_z.at[i], dst_ref=scan_rz.at[i], send_sem=scan_send.at[i, 1], recv_sem=scan_recv.at[i, 1],
            device_id={"wide": jnp.maximum(w - s, 0)}, device_id_type=MESH,
        )
        scans.append((right, left, s))

        @pl.when(w < n_w - s)
        def _():
            right.start()

        @pl.when(w >= s)
        def _():
            left.start()

        if i == 0:
            start("coarse")
            start("u2")
            pack[2] = jnp.where(inner, second[:, :128], second[:, 128:])
            start("u2corner")

        @pl.when(w >= s)
        def _():
            right.wait_recv()

        @pl.when(w < n_w - s)
        def _():
            left.wait_recv()

        got_f, got_z = scan_rf[i], scan_rz[i]
        forward = forward + step_all * got_f
        backward = backward + step_all * got_z
        if i:
            enter = enter + (got_f if i == 1 else step_less * got_f)
            leave = leave + (got_z if i == 1 else step_less * got_z)
            step_less = step_all if i == 1 else step_less * step_all
        step_all = step_all * step_all

    arrive("coarse")
    window = range(-4, cx + 4)
    causal = {-5: enter}
    beyond = {cx + 3: r * leave}
    total = enter * jnp.where(is_last, power[2 * cx + 2], far * power[2 * cx + 6])
    for t in window:
        value = coarse[4 + t]
        causal[t] = value + r * causal[t - 1]
        total = total + value * jnp.where(is_last, power[max(cx + 1 - t, 0)], far * power[2 * cx + 1 - t])
    for t in reversed(range(-4, cx + 3)):
        beyond[t] = r * (beyond[t + 1] + coarse[4 + t + 1])
    for t in range(-3, cx + 3):
        back = jnp.where(is_last, power[max(cx - 1 - t, 0)], power[cx + 3 - t])
        value = scale * (causal[t] + beyond[t] - back * total)
        if t < 0:
            value = jnp.where(w == 0, 0.0, value)
        if t >= cx:
            value = jnp.where(is_last, 0.0, value)
        line[4 + t] = value
    pack_c = packed([(t + 3, coarse[4 + t]) for t in range(-3, cx + 3)])
    pack_l = packed([(t + 3, line[4 + t]) for t in range(-3, cx + 3)])
    pack[3] = pack_c
    pack[4] = pack_l
    start("line")

    arrive("u2", "u2corner")
    halo = jnp.where(
        row_c < own - 1, pltpu.roll(corner[1, 0], 64, 1),
        jnp.where(row_c > own + nx, pltpu.roll(corner[1, 1], 64, 1), pack[2]),
    )
    second = strips(packed([(e, u2[e]) for e in range(nx + 6)]), halo, halo)

    arrive("line")
    c_sides = strips(pack_c, strip[2], strip[4])
    l_sides = strips(pack_l, strip[3], strip[5])

    def correction(x):
        v = line[4 + x]
        nb = line[3 + x] + line[5 + x] + sides(v, l_sides, x + 3)
        a = coef[x][:1]
        return exact(0.6 * v + apply(coarse[4 + x] + (4.0 - 4.0 * a) * v + a * nb), spread)

    for x in range(-2, cx + 2):
        value = correction(x)
        for e in (own + 2 * x, own + 2 * x + 1):
            if 0 <= e < nx + 6:
                u3[e] = u2[e] + value
    fix = smooth_strip(l_sides, c_sides, c_strip)
    fix = exact(jnp.concatenate([fix[:, :128], fix[:, 128:]], axis=0), spread_strip)
    third = second + jnp.concatenate([fix[:levels], fix[levels:]], axis=1)
    for e in range(1, nx + 5):
        u4[e] = smooth(u3, third, e)
    fourth = smooth_strip(third, rhs_strip, a_strip)
    for e in range(2, nx + 4):
        p[e] = smooth(u4, fourth, e)
    fifth = smooth_strip(fourth, rhs_strip, a_strip)
    for x in range(nx):
        u, h = horizontal(p, fifth, own + x)
        p_out[:, x, :] = u
        r_out[:, x, :] = h - vertical(u)

    for name in names:
        for copy, goes, _ in copies(name):
            @pl.when(goes)
            def _():
                copy.wait_send()
    for right, left, s in scans:
        @pl.when(w < n_w - s)
        def _():
            right.wait_send()

        @pl.when(w >= s)
        def _():
            left.wait_send()


def local(n_w, n_n, rhs, areas, stiffness):
    levels, nx, ny = rhs.shape
    cx = nx // 2
    steps = max(1, (n_w - 1).bit_length())
    vmem = lambda *shape: pltpu.VMEM(shape, f32)
    whole = pl.BlockSpec(memory_space=pltpu.VMEM)
    return pl.pallas_call(
        functools.partial(kernel, n_w, n_n, nx, ny, levels),
        out_shape=[jax.ShapeDtypeStruct(rhs.shape, f32)] * 2,
        in_specs=[whole, whole, pl.BlockSpec(memory_space=pltpu.SMEM)],
        out_specs=[whole, whole],
        scratch_shapes=[vmem(nx + 6, levels, ny)] * 6
        + [
            vmem(3 * nx, ny), vmem(cx + 8, levels, 128), vmem(cx + 8, levels, 128),
            vmem(5, levels, 128), vmem(6, levels, 128), vmem(2, 2, levels, 128),
            vmem(16, 128), vmem(2, 16, 128),
            vmem(steps, levels, 128), vmem(steps, levels, 128),
            vmem(steps, levels, 128), vmem(steps, levels, 128),
            vmem(levels, 128), vmem(levels, 128), vmem(levels, 128),
            pltpu.SemaphoreType.DMA((9, 2)), pltpu.SemaphoreType.DMA((9, 2)),
            pltpu.SemaphoreType.DMA((steps, 2)), pltpu.SemaphoreType.DMA((steps, 2)),
        ],
        compiler_params=pltpu.CompilerParams(
            collective_id=0, has_side_effects=True, vmem_limit_bytes=40 * 1024 * 1024
        ),
        cost_estimate=pl.CostEstimate(flops=80_000_000, bytes_accessed=1_600_000, transcendentals=0),
    )(rhs, areas, stiffness)


def solution(mesh):
    placed = (P(None, "wide", "narrow"), P("wide", "narrow"), P())
    return jax.shard_map(
        functools.partial(local, mesh.shape["wide"], mesh.shape["narrow"]),
        mesh=mesh,
        in_specs=placed,
        out_specs=(P(None, "wide", "narrow"), P(None, "wide", "narrow")),
        check_vma=False,
    )
```

```python
import functools

import jax
import jax.numpy as jnp
from jax import lax
from jax.experimental import pallas as pl
from jax.experimental.pallas import tpu as pltpu
from jax.sharding import PartitionSpec as P

MESH = pl.DeviceIdType.MESH
f32 = jnp.float32
bf16 = jnp.bfloat16


def halves(value):
    high = value.astype(bf16)
    return high, (value - high.astype(f32)).astype(bf16)


def kernel(
    n_w, n_n, nx, ny, levels,
    rhs_ref, areas_ref, stiff_ref, p_out, r_out,
    rhs_x, u1, u2, u3, u4, p, wide_a, coarse, line, pack, strip, corner, pack_a, strip_a, coef_at,
    scan_f, scan_z, scan_rf, scan_rz, theta, phi, stiff_b,
    send_sem, recv_sem, scan_send, scan_recv,
):
    cx, cy = nx // 2, ny // 2
    w, c = lax.axis_index("wide"), lax.axis_index("narrow")
    has = (w > 0, w < n_w - 1, c > 0, c < n_n - 1)
    to = (
        {"wide": jnp.maximum(w - 1, 0)},
        {"wide": jnp.minimum(w + 1, n_w - 1)},
        {"narrow": jnp.maximum(c - 1, 0)},
        {"narrow": jnp.minimum(c + 1, n_n - 1)},
    )
    strides = []
    while (1 << len(strides)) < n_w:
        strides.append(1 << len(strides))
    own = 3
    tiles = ny // 128

    small = jnp.zeros((levels, 128), f32)
    nothing = jnp.zeros((levels, ny), f32)
    edge_x = (
        ((1, 2), (0, 1), (0, 1, 2, 3)),
        ((nx + 3, nx + 4), (nx + 4, nx + 5), (cx + 4, cx + 5, cx + 6, cx + 7)),
    )
    for side in range(2):
        @pl.when(jnp.logical_not(has[side]))
        def _():
            for e in edge_x[side][0]:
                rhs_x[e + 1] = nothing
            for e in edge_x[side][1]:
                u2[e + 1] = nothing
            for e in edge_x[side][2]:
                coarse[e] = small
            corner[0, side] = small
            corner[1, side] = small
            wide_a[2 * side * nx : 2 * side * nx + nx, :] = jnp.zeros((nx, ny), f32)

        @pl.when(jnp.logical_not(has[2 + side]))
        def _():
            strip[side] = small
            strip[2 + 2 * side] = small
            strip[3 + 2 * side] = small
            strip_a[side] = jnp.zeros((16, 128), f32)
    for i, s in enumerate(strides):
        @pl.when(w < s)
        def _():
            scan_rf[i] = small

        @pl.when(w >= n_w - s)
        def _():
            scan_rz[i] = small

    barrier = pltpu.get_barrier_semaphore()
    for side in range(4):
        @pl.when(has[side])
        def _():
            pl.semaphore_signal(barrier, inc=1, device_id=to[side], device_id_type=MESH)
    for s in strides[1:]:
        @pl.when(w >= s)
        def _():
            pl.semaphore_signal(
                barrier, inc=1, device_id={"wide": jnp.maximum(w - s, 0)}, device_id_type=MESH
            )

        @pl.when(w < n_w - s)
        def _():
            pl.semaphore_signal(
                barrier, inc=1, device_id={"wide": jnp.minimum(w + s, n_w - 1)}, device_id_type=MESH
            )

    exchanges = {
        "areas": (0, (wide_a.at[pl.ds(nx, nx)], wide_a.at[pl.ds(2 * nx, nx)]),
                  (wide_a.at[pl.ds(nx, nx)], wide_a.at[pl.ds(0, nx)])),
        "rhs": (0, (rhs_x.at[pl.ds(own + 1, 2)], rhs_x.at[pl.ds(own + nx + 1, 2)]),
                (rhs_x.at[pl.ds(own + nx - 2 + 1, 2)], rhs_x.at[pl.ds(own - 2 + 1, 2)])),
        "corner": (0, (pack.at[1], corner.at[0, 1]), (pack.at[1], corner.at[0, 0])),
        "u2": (0, (u2.at[pl.ds(own + 1 + 1, 2)], u2.at[pl.ds(own + nx + 1 + 1, 2)]),
               (u2.at[pl.ds(own + nx - 3 + 1, 2)], u2.at[pl.ds(own - 3 + 1, 2)])),
        "u2corner": (0, (pack.at[2], corner.at[1, 1]), (pack.at[2], corner.at[1, 0])),
        "coarse": (0, (coarse.at[pl.ds(4, cx)], coarse.at[pl.ds(4 + cx, cx)]),
                   (coarse.at[pl.ds(4, cx)], coarse.at[pl.ds(4 - cx, cx)])),
        "strip": (1, (pack.at[0], strip.at[1]), (pack.at[0], strip.at[0])),
        "strip_a": (1, (pack_a, strip_a.at[1]), (pack_a, strip_a.at[0])),
        "line": (1, (pack.at[pl.ds(3, 2)], strip.at[pl.ds(4, 2)]), (pack.at[pl.ds(3, 2)], strip.at[pl.ds(2, 2)])),
    }
    names = list(exchanges)

    def copies(name):
        axis, low, high = exchanges[name]
        at = names.index(name)
        return [
            (
                pltpu.make_async_remote_copy(
                    src_ref=pair[0], dst_ref=pair[1], send_sem=send_sem.at[at, i], recv_sem=recv_sem.at[at, i],
                    device_id=to[2 * axis + i], device_id_type=MESH,
                ),
                has[2 * axis + i],
                has[2 * axis + 1 - i],
            )
            for i, pair in enumerate((low, high))
        ]

    def start(name):
        for copy, goes, _ in copies(name):
            @pl.when(goes)
            def _():
                copy.start()

    def arrive(*which):
        for name in which:
            for copy, _, comes in copies(name):
                @pl.when(comes)
                def _():
                    copy.wait_recv()

    lane = lax.broadcasted_iota(jnp.int32, (levels, ny), 1)
    lane_c = lax.broadcasted_iota(jnp.int32, (levels, 128), 1)
    level = lax.broadcasted_iota(jnp.int32, (levels, ny), 0)
    inner = lane_c % 8 < 4
    row_c = lane_c // 8

    def packed(get, start_at, stop_at, base=None):
        def body(e, result):
            value = get(e)
            ends = jnp.where(lane_c < 4, value[:, :128], value[:, value.shape[1] - 128 :])
            return jnp.where(row_c == e, pltpu.roll(ends, 8 * e + 4, 1), result)

        return lax.fori_loop(start_at, stop_at, body, jnp.zeros((levels, 128), f32) if base is None else base, unroll=2)

    def pairs(count, body):
        def both(i, carry):
            body(2 * i)
            body(2 * i + 1)
            return carry

        lax.fori_loop(0, count // 2, both, 0)

    def strips(mine, low, high):
        return jnp.concatenate([jnp.where(inner, low, mine), jnp.where(inner, mine, high)], axis=1)

    wide_a[nx : 2 * nx, :] = areas_ref[...]
    for x in (0, 1, nx - 2, nx - 1) + tuple(range(2, nx - 2)):
        rhs_x[own + x + 1] = jnp.concatenate(
            [rhs_ref[pl.ds(x + nx * t, levels, stride=tiles * nx), :] for t in range(tiles)], axis=1
        )
    peers = sum(h.astype(jnp.int32) for h in has)
    for s in strides[1:]:
        peers = peers + (w >= s).astype(jnp.int32) + (w < n_w - s).astype(jnp.int32)
    pl.semaphore_wait(barrier, peers)
    start("areas")
    start("rhs")
    pack_rhs = packed(lambda e: rhs_x[e + 1], own, own + nx)
    pack[0] = pack_rhs
    start("strip")

    def minors(i, carry):
        t_before, t_now, p_before, p_now = carry
        j = levels - 1 - i
        here, there = stiff_ref[i], stiff_ref[j]
        theta[pl.ds(i, 1), :] = jnp.full((1, 128), t_now, f32)
        phi[pl.ds(j, 1), :] = jnp.full((1, 128), p_now, f32)
        stiff_b[pl.ds(i, 1), :] = jnp.full((1, 128), here, f32)
        return (
            t_now, (here * 0.125 + 1.0) * t_now - 0.0625 * t_before,
            p_now, (there * 0.125 + 1.0) * p_now - 0.0625 * p_before,
        )

    zero, one = jnp.float32(0.0), jnp.float32(1.0)
    now = lax.fori_loop(0, levels, minors, (zero, one, zero, one), unroll=8)[1]
    whole = jnp.full((levels, 128), now, f32)
    row = lax.broadcasted_iota(jnp.int32, (levels, 128), 0)
    col = lax.broadcasted_iota(jnp.int32, (levels, 128), 1)
    apart = jnp.abs(row - col)
    decay = jnp.full((levels, 128), 0.4 * 0.125, f32)
    for b in range(6):
        decay = jnp.where((apart & (1 << b)) != 0, decay * (0.25 ** (1 << b)), decay)
    t_col, p_col = theta[...], phi[...]
    same = row == col
    t_row = jnp.sum(jnp.where(same, t_col, 0.0), axis=0, keepdims=True)
    p_row = jnp.sum(jnp.where(same, p_col, 0.0), axis=0, keepdims=True)
    inverse = (jnp.where(row <= col, t_col * p_row, p_col * t_row) * decay / whole)[:, :levels]
    inv_hi, inv_lo = halves(inverse)
    weights = jnp.concatenate([inv_hi, inv_hi, inv_lo], axis=1)

    def apply(value):
        high, low = halves(value)
        stacked = jnp.concatenate([high, low, high], axis=0)
        return jnp.dot(weights, stacked, preferred_element_type=f32)

    def area(e):
        return wide_a[pl.ds(nx + e - own, 1), :]

    def sides(u, sides_of, e):
        n = u.shape[1]
        index = lane[:, :n]
        low = pltpu.roll(sides_of[:, :128], (125 - 8 * e) % 128, 1)
        high = pltpu.roll(sides_of[:, 128:], (123 - 8 * e) % 128, 1)
        if n == 128:
            down = jnp.where(index == 0, low, pltpu.roll(u, 1, 1))
            return down + jnp.where(index == n - 1, high, pltpu.roll(u, n - 1, 1))
        edge = jnp.concatenate([low, high], axis=1)
        down = jnp.where(index == 0, edge, pltpu.roll(u, 1, 1))
        return down + jnp.where(index == n - 1, edge, pltpu.roll(u, n - 1, 1))

    def smooth(field, sides_of, e):
        u = field[e + 1]
        nb = field[e] + field[e + 2] + sides(u, sides_of, e)
        a = area(e)
        return 0.6 * u + apply(rhs_x[e + 1] + (4.0 - 4.0 * a) * u + a * nb)

    def smooth_strip(s, right_side, a):
        nb = pltpu.roll(s, 1, 1) + pltpu.roll(s, ny - 1, 1) + pltpu.roll(s, 8, 1) + pltpu.roll(s, ny - 8, 1)
        return 0.6 * s + apply(right_side + (4.0 - 4.0 * a) * s + a * nb)

    def horizontal(field, sides_of, e):
        u = field[e + 1]
        nb = field[e] + field[e + 2] + sides(u, sides_of, e)
        return u, rhs_x[e + 1] - area(e) * (4.0 * u - nb)

    def vertical(v):
        above = jnp.where(level == levels - 1, 0.0, pltpu.roll(v, levels - 1, 0))
        below = jnp.where(level == 0, 0.0, pltpu.roll(v, 1, 0))
        s = jnp.concatenate([stiff_b[...]] * (ny // 128), axis=1)
        return (s + 4.0) * v - 2.0 * (above + below)

    pick = jnp.where(
        lax.broadcasted_iota(jnp.int32, (ny, cy), 0) // 2 == lax.broadcasted_iota(jnp.int32, (ny, cy), 1),
        1.0, 0.0,
    ).astype(bf16)
    spread = jnp.where(
        lax.broadcasted_iota(jnp.int32, (cy, ny), 1) // 2 == lax.broadcasted_iota(jnp.int32, (cy, ny), 0),
        1.0, 0.0,
    ).astype(bf16)
    fine_lane = lax.broadcasted_iota(jnp.int32, (128, 128), 1)
    spread_strip = jnp.where(
        lax.broadcasted_iota(jnp.int32, (128, 128), 0)
        == 8 * ((fine_lane // 8 + 3) // 2) + 2 + (fine_lane % 8) // 2,
        1.0, 0.0,
    ).astype(bf16)

    def exact(value, matrix):
        rows = value.shape[0]
        high, low = halves(value)
        both = jnp.dot(jnp.concatenate([high, low], axis=0), matrix, preferred_element_type=f32)
        return both[:rows] + both[rows:]

    def first_own(i):
        u1[own + i + 1] = apply(rhs_x[own + i + 1])

    pairs(nx, first_own)

    arrive("strip")
    halo = jnp.where(inner, strip[0], strip[1])
    pack[1] = halo
    start("corner")
    first = apply(strips(pack_rhs, halo, halo))
    first_own_strip = first

    def second_own(i):
        e = own + 1 + i
        u2[e + 1] = smooth(u1, first_own_strip, e)

    pairs(nx - 2, second_own)

    arrive("areas")
    eight = lane_c[:8]

    def put_area(e, result):
        v = jnp.broadcast_to(area(e), (8, ny))
        v = pltpu.roll(jnp.where(eight < 4, v[:, :128], v[:, ny - 128 :]), 8 * e + 4, 1)
        return jnp.where(eight // 8 == e, v, result)

    packed_a = lax.fori_loop(0, nx + 6, put_area, jnp.zeros((8, 128), f32), unroll=2)
    sums = []
    for x in range(-2, cx + 2):
        at = nx + 2 * x
        sums.append(jnp.broadcast_to(0.0625 * (wide_a[at : at + 1, :] + wide_a[at + 1 : at + 2, :]), (8, ny)))
    coef = exact(jnp.concatenate(sums, axis=0), pick)
    for x in range(cx + 4):
        coef_at[x] = coef[8 * x : 8 * x + 8]
    coef = {x: coef[8 * (x + 2) : 8 * (x + 2) + 8] for x in range(-2, cx + 2)}
    packed_c = jnp.zeros((8, 128), f32)
    for x in range(-2, cx + 2):
        v = pltpu.roll(coef[x], 8 * (x + 3) + 4, 1)
        packed_c = jnp.where(eight // 8 == x + 3, v, packed_c)
    pack_a[0:8, :] = packed_a
    pack_a[8:16, :] = packed_c
    start("strip_a")

    arrive("rhs")
    def first_outer(i):
        e = own - 2 + i % 2 + (nx + 2) * (i // 2)
        u1[e + 1] = apply(rhs_x[e + 1])

    pairs(4, first_outer)
    pack_all = packed(lambda e: rhs_x[e + 1], own - 2, own, pack_rhs)
    pack_all = packed(lambda e: rhs_x[e + 1], own + nx, own + nx + 2, pack_all)
    arrive("corner", "strip_a")
    halo = jnp.where(
        row_c < own, pltpu.roll(corner[0, 0], 64, 1),
        jnp.where(row_c >= own + nx, pltpu.roll(corner[0, 1], 64, 1), halo),
    )
    rhs_strip = strips(pack_all, halo, halo)
    inner_a = eight % 8 < 4

    def strips_a(low, high, mine):
        return jnp.concatenate([jnp.where(inner_a, low, mine), jnp.where(inner_a, mine, high)], axis=1)[:1]

    a_strip = strips_a(strip_a[0, 0:8, :], strip_a[1, 0:8, :], packed_a)
    c_strip = strips_a(strip_a[0, 8:16, :], strip_a[1, 8:16, :], packed_c)
    first = apply(rhs_strip)

    def second_outer(i):
        e = own - 1 + i % 2 + nx * (i // 2)
        u2[e + 1] = smooth(u1, first, e)

    pairs(4, second_outer)
    second = smooth_strip(first, rhs_strip, a_strip)

    s = stiff_b[...]
    keep = jnp.sqrt(s + 0.25 * s * s) - 0.5 * s
    r = 1.0 - keep
    power = [jnp.ones_like(r)]
    for _ in range(4 * cx):
        power.append(power[-1] * r)
    is_last = w == n_w - 1
    far = jnp.ones_like(r)
    base = power[2 * cx]
    steps = jnp.maximum(n_w - 2 - w, 0)
    for b in range(len(strides)):
        far = jnp.where((steps >> b) % 2 == 1, far * base, far)
        base = base * base
    tail = jnp.where(is_last, power[0], far * power[2 * cx])
    scale = keep / (1.0 + r)

    def to_coarse(x):
        e = own + 2 * x
        u_a, h_a = horizontal(u2, second, e)
        u_b, h_b = horizontal(u2, second, e + 1)
        coarse[4 + x] = exact(0.25 * (h_a + h_b - vertical(u_a + u_b)), pick)

    pairs(cx, to_coarse)
    mine = [coarse[4 + x] for x in range(cx)]
    forward = mine[0]
    for x in range(1, cx):
        forward = mine[x] + r * forward
    backward = sum((power[x] - tail * power[2 * cx - x]) * mine[x] for x in range(cx))
    enter = jnp.zeros_like(forward)
    leave = jnp.zeros_like(forward)
    step_all = power[cx]
    step_less = None
    scans = []
    for i, s in enumerate(strides):
        scan_f[i] = forward
        scan_z[i] = backward
        right = pltpu.make_async_remote_copy(
            src_ref=scan_f.at[i], dst_ref=scan_rf.at[i], send_sem=scan_send.at[i, 0], recv_sem=scan_recv.at[i, 0],
            device_id={"wide": jnp.minimum(w + s, n_w - 1)}, device_id_type=MESH,
        )
        left = pltpu.make_async_remote_copy(
            src_ref=scan_z.at[i], dst_ref=scan_rz.at[i], send_sem=scan_send.at[i, 1], recv_sem=scan_recv.at[i, 1],
            device_id={"wide": jnp.maximum(w - s, 0)}, device_id_type=MESH,
        )
        scans.append((right, left, s))

        @pl.when(w < n_w - s)
        def _():
            right.start()

        @pl.when(w >= s)
        def _():
            left.start()

        if i == 0:
            start("coarse")
            start("u2")
            pack[2] = jnp.where(inner, second[:, :128], second[:, 128:])
            start("u2corner")

        @pl.when(w >= s)
        def _():
            right.wait_recv()

        @pl.when(w < n_w - s)
        def _():
            left.wait_recv()

        got_f, got_z = scan_rf[i], scan_rz[i]
        forward = forward + step_all * got_f
        backward = backward + step_all * got_z
        if i:
            enter = enter + (got_f if i == 1 else step_less * got_f)
            leave = leave + (got_z if i == 1 else step_less * got_z)
            step_less = step_all if i == 1 else step_less * step_all
        step_all = step_all * step_all

    arrive("coarse")
    window = range(-4, cx + 4)
    causal = {-5: enter}
    beyond = {cx + 3: r * leave}
    total = enter * jnp.where(is_last, power[2 * cx + 2], far * power[2 * cx + 6])
    for t in window:
        value = coarse[4 + t]
        causal[t] = value + r * causal[t - 1]
        total = total + value * jnp.where(is_last, power[max(cx + 1 - t, 0)], far * power[2 * cx + 1 - t])
    for t in reversed(range(-4, cx + 3)):
        beyond[t] = r * (beyond[t + 1] + coarse[4 + t + 1])
    for t in range(-3, cx + 3):
        back = jnp.where(is_last, power[max(cx - 1 - t, 0)], power[cx + 3 - t])
        value = scale * (causal[t] + beyond[t] - back * total)
        if t < 0:
            value = jnp.where(w == 0, 0.0, value)
        if t >= cx:
            value = jnp.where(is_last, 0.0, value)
        line[4 + t] = value
    pack_c = packed(lambda e: coarse[e + 1], 0, cx + 6)
    pack_l = packed(lambda e: line[e + 1], 0, cx + 6)
    pack[3] = pack_c
    pack[4] = pack_l
    start("line")

    arrive("u2", "u2corner")
    halo = jnp.where(
        row_c < own - 1, pltpu.roll(corner[1, 0], 64, 1),
        jnp.where(row_c > own + nx, pltpu.roll(corner[1, 1], 64, 1), pack[2]),
    )
    second = strips(packed(lambda e: u2[e + 1], 0, nx + 6), halo, halo)

    arrive("line")
    c_sides = strips(pack_c, strip[2], strip[4])
    l_sides = strips(pack_l, strip[3], strip[5])

    def correction(x):
        v = line[4 + x]
        nb = line[3 + x] + line[5 + x] + sides(v, l_sides, x + 3)
        a = coef_at[x + 2][:1]
        return exact(0.6 * v + apply(coarse[4 + x] + (4.0 - 4.0 * a) * v + a * nb), spread)

    def third_rows(i):
        value = correction(i - 2)
        for e in (own + 2 * i - 4, own + 2 * i - 3):
            u3[e + 1] = u2[e + 1] + value

    pairs(cx + 4, third_rows)
    fix = smooth_strip(l_sides, c_sides, c_strip)
    fix = exact(jnp.concatenate([fix[:, :128], fix[:, 128:]], axis=0), spread_strip)
    third = second + jnp.concatenate([fix[:levels], fix[levels:]], axis=1)

    def fourth_rows(i):
        u4[i + 2] = smooth(u3, third, i + 1)

    pairs(nx + 4, fourth_rows)
    fourth = smooth_strip(third, rhs_strip, a_strip)

    def fifth_rows(i):
        p[i + 3] = smooth(u4, fourth, i + 2)

    pairs(nx + 2, fifth_rows)
    fifth = smooth_strip(fourth, rhs_strip, a_strip)

    def last_rows(x):
        u, h = horizontal(p, fifth, own + x)
        left_over = h - vertical(u)
        for t in range(tiles):
            at = pl.ds(x + nx * t, levels, stride=tiles * nx)
            p_out[at, :] = u[:, 128 * t : 128 * t + 128]
            r_out[at, :] = left_over[:, 128 * t : 128 * t + 128]

    pairs(nx, last_rows)

    for name in names:
        for copy, goes, _ in copies(name):
            @pl.when(goes)
            def _():
                copy.wait_send()
    for right, left, s in scans:
        @pl.when(w < n_w - s)
        def _():
            right.wait_send()

        @pl.when(w >= s)
        def _():
            left.wait_send()


def local(n_w, n_n, rhs, areas, stiffness):
    levels, nx, ny = rhs.shape
    cx, tiles = nx // 2, ny // 128
    steps = max(1, (n_w - 1).bit_length())
    vmem = lambda *shape: pltpu.VMEM(shape, f32)
    whole = pl.BlockSpec(memory_space=pltpu.VMEM)
    outs = pl.pallas_call(
        functools.partial(kernel, n_w, n_n, nx, ny, levels),
        out_shape=[jax.ShapeDtypeStruct((levels * nx * tiles, 128), f32)] * 2,
        in_specs=[whole, whole, pl.BlockSpec(memory_space=pltpu.SMEM)],
        out_specs=[whole, whole],
        scratch_shapes=[vmem(nx + 8, levels, ny)] * 6
        + [
            vmem(3 * nx, ny), vmem(cx + 8, levels, 128), vmem(cx + 8, levels, 128),
            vmem(5, levels, 128), vmem(6, levels, 128), vmem(2, 2, levels, 128),
            vmem(16, 128), vmem(2, 16, 128), vmem(cx + 4, 8, 128),
            vmem(steps, levels, 128), vmem(steps, levels, 128),
            vmem(steps, levels, 128), vmem(steps, levels, 128),
            vmem(levels, 128), vmem(levels, 128), vmem(levels, 128),
            pltpu.SemaphoreType.DMA((9, 2)), pltpu.SemaphoreType.DMA((9, 2)),
            pltpu.SemaphoreType.DMA((steps, 2)), pltpu.SemaphoreType.DMA((steps, 2)),
        ],
        compiler_params=pltpu.CompilerParams(
            collective_id=0, has_side_effects=True, vmem_limit_bytes=40 * 1024 * 1024
        ),
        cost_estimate=pl.CostEstimate(flops=80_000_000, bytes_accessed=1_600_000, transcendentals=0),
    )(rhs.reshape(levels, nx, tiles, 128).transpose(0, 2, 1, 3).reshape(-1, 128), areas, stiffness)
    return tuple(v.reshape(levels, tiles, nx, 128).transpose(0, 2, 1, 3).reshape(rhs.shape) for v in outs)


def solution(mesh):
    placed = (P(None, "wide", "narrow"), P("wide", "narrow"), P())
    return jax.shard_map(
        functools.partial(local, mesh.shape["wide"], mesh.shape["narrow"]),
        mesh=mesh,
        in_specs=placed,
        out_specs=(P(None, "wide", "narrow"), P(None, "wide", "narrow")),
        check_vma=False,
    )
```

```python
import functools

import jax
import jax.numpy as jnp
from jax import lax
from jax.experimental import pallas as pl
from jax.experimental.pallas import tpu as pltpu
from jax.sharding import PartitionSpec as P

MESH = pl.DeviceIdType.MESH
f32 = jnp.float32
bf16 = jnp.bfloat16


def halves(value):
    high = value.astype(bf16)
    return high, (value - high.astype(f32)).astype(bf16)


def kernel(
    n_w, n_n, nx, ny, levels,
    rhs_ref, areas_ref, stiff_ref, p_out, r_out,
    rhs_x, u1, u2, u3, u4, p, wide_a, coarse, line, pack, strip, corner_of, corner, pack_a, strip_a,
    scan_f, scan_z, scan_rf, scan_rz, theta, phi, stiff_b,
    send_sem, recv_sem, scan_send, scan_recv,
):
    cx, cy = nx // 2, ny // 2
    w, c = lax.axis_index("wide"), lax.axis_index("narrow")
    has = (w > 0, w < n_w - 1, c > 0, c < n_n - 1)
    to = (
        {"wide": jnp.maximum(w - 1, 0)},
        {"wide": jnp.minimum(w + 1, n_w - 1)},
        {"narrow": jnp.maximum(c - 1, 0)},
        {"narrow": jnp.minimum(c + 1, n_n - 1)},
    )
    strides = []
    while (1 << len(strides)) < n_w:
        strides.append(1 << len(strides))
    own = 3
    tiles = ny // 128

    small = jnp.zeros((levels, 128), f32)
    nothing = jnp.zeros((levels, ny), f32)
    edge_x = (
        ((1, 2), (0, 1), (2, 3)),
        ((nx + 3, nx + 4), (nx + 4, nx + 5), (cx + 4, cx + 5)),
    )
    rhs_x[0] = nothing
    rhs_x[nx + 5] = nothing
    for side in range(2):
        @pl.when(jnp.logical_not(has[side]))
        def _():
            for e in edge_x[side][0]:
                rhs_x[e] = nothing
            for e in edge_x[side][1]:
                u2[e] = nothing
            for e in edge_x[side][2]:
                coarse[e] = small
            corner[0, side] = small[:8]
            corner[1, side] = small[:8]
            wide_a[2 * side * nx : 2 * side * nx + nx, :] = jnp.zeros((nx, ny), f32)

        @pl.when(jnp.logical_not(has[2 + side]))
        def _():
            strip[side] = small
            strip[2 + 2 * side] = small
            strip[3 + 2 * side] = small
            strip_a[side] = jnp.zeros((16, 128), f32)
    for i, s in enumerate(strides):
        @pl.when(w < s)
        def _():
            scan_rf[i] = small

        @pl.when(w >= n_w - s)
        def _():
            scan_rz[i] = small

    barrier = pltpu.get_barrier_semaphore()
    for side in range(4):
        @pl.when(has[side])
        def _():
            pl.semaphore_signal(barrier, inc=1, device_id=to[side], device_id_type=MESH)
    for s in strides[1:]:
        @pl.when(w >= s)
        def _():
            pl.semaphore_signal(
                barrier, inc=1, device_id={"wide": jnp.maximum(w - s, 0)}, device_id_type=MESH
            )

        @pl.when(w < n_w - s)
        def _():
            pl.semaphore_signal(
                barrier, inc=1, device_id={"wide": jnp.minimum(w + s, n_w - 1)}, device_id_type=MESH
            )

    exchanges = {
        "areas": (0, (wide_a.at[pl.ds(nx, nx)], wide_a.at[pl.ds(2 * nx, nx)]),
                  (wide_a.at[pl.ds(nx, nx)], wide_a.at[pl.ds(0, nx)])),
        "rhs": (0, (rhs_x.at[pl.ds(own, 2)], rhs_x.at[pl.ds(own + nx, 2)]),
                (rhs_x.at[pl.ds(own + nx - 2, 2)], rhs_x.at[pl.ds(own - 2, 2)])),
        "corner": (0, (corner_of.at[0, 0], corner.at[0, 1]), (corner_of.at[0, 1], corner.at[0, 0])),
        "u2near": (0, (u2.at[own + 1], u2.at[own + nx + 1]), (u2.at[own + nx - 2], u2.at[own - 2])),
        "u2far": (0, (u2.at[own + 2], u2.at[own + nx + 2]), (u2.at[own + nx - 3], u2.at[own - 3])),
        "u2corner": (0, (corner_of.at[1, 0], corner.at[1, 1]), (corner_of.at[1, 1], corner.at[1, 0])),
        "coarse": (0, (coarse.at[pl.ds(4, 2)], coarse.at[pl.ds(4 + cx, 2)]),
                   (coarse.at[pl.ds(2 + cx, 2)], coarse.at[pl.ds(2, 2)])),
        "strip": (1, (pack.at[0], strip.at[1]), (pack.at[0], strip.at[0])),
        "strip_a": (1, (pack_a, strip_a.at[1]), (pack_a, strip_a.at[0])),
        "line": (1, (pack.at[pl.ds(1, 2)], strip.at[pl.ds(4, 2)]), (pack.at[pl.ds(1, 2)], strip.at[pl.ds(2, 2)])),
    }
    names = list(exchanges)

    def copies(name):
        axis, low, high = exchanges[name]
        at = names.index(name)
        return [
            (
                pltpu.make_async_remote_copy(
                    src_ref=pair[0], dst_ref=pair[1], send_sem=send_sem.at[at, i], recv_sem=recv_sem.at[at, i],
                    device_id=to[2 * axis + i], device_id_type=MESH,
                ),
                has[2 * axis + i],
                has[2 * axis + 1 - i],
            )
            for i, pair in enumerate((low, high))
        ]

    def start(name):
        for copy, goes, _ in copies(name):
            @pl.when(goes)
            def _():
                copy.start()

    def arrive(*which):
        for name in which:
            for copy, _, comes in copies(name):
                @pl.when(comes)
                def _():
                    copy.wait_recv()

    lane = lax.broadcasted_iota(jnp.int32, (levels, ny), 1)
    lane_c = lax.broadcasted_iota(jnp.int32, (levels, 128), 1)
    level = lax.broadcasted_iota(jnp.int32, (levels, ny), 0)
    inner = lane_c % 8 < 4
    row_c = lane_c // 8

    def packed(rows, base=None):
        result = jnp.zeros((levels, 128), f32) if base is None else base
        for e, value in rows:
            ends = jnp.where(lane_c < 4, value[:, :128], value[:, value.shape[1] - 128 :])
            result = jnp.where(row_c == e, pltpu.roll(ends, 8 * e + 4, 1), result)
        return result

    def strips(mine, low, high):
        return jnp.concatenate([jnp.where(inner, low, mine), jnp.where(inner, mine, high)], axis=1)

    def squeeze(tile, e):
        result = jnp.zeros((8, 128), f32)
        for b in range(levels // 8):
            part = pltpu.roll(tile[8 * b : 8 * b + 8], (16 * b - 8 * e) % 128, 1)
            result = jnp.where(lane_c[:8] // 16 == b, part, result)
        return result

    def unsqueeze(tile, e):
        return jnp.concatenate([pltpu.roll(tile, (8 * e - 16 * b) % 128, 1) for b in range(levels // 8)], axis=0)

    wide_a[nx : 2 * nx, :] = areas_ref[...]
    for x in (0, 1, nx - 2, nx - 1) + tuple(range(2, nx - 2)):
        rhs_x[own + x] = jnp.concatenate(
            [rhs_ref[pl.ds(x + nx * t, levels, stride=tiles * nx), :] for t in range(tiles)], axis=1
        )
    peers = sum(h.astype(jnp.int32) for h in has)
    for s in strides[1:]:
        peers = peers + (w >= s).astype(jnp.int32) + (w < n_w - s).astype(jnp.int32)
    pl.semaphore_wait(barrier, peers)
    start("areas")
    start("rhs")
    pack_rhs = packed([(e, rhs_x[e]) for e in range(own, own + nx)])
    pack[0] = pack_rhs
    start("strip")

    zero, one = jnp.float32(0.0), jnp.float32(1.0)
    t_before, t_now, p_before, p_now = zero, one, zero, one
    for i in range(levels):
        j = levels - 1 - i
        here, there = stiff_ref[i], stiff_ref[j]
        theta[i : i + 1, :] = jnp.full((1, 128), t_now, f32)
        phi[j : j + 1, :] = jnp.full((1, 128), p_now, f32)
        stiff_b[i : i + 1, :] = jnp.full((1, 128), here, f32)
        t_before, t_now = t_now, (here * 0.125 + 1.0) * t_now - 0.0625 * t_before
        p_before, p_now = p_now, (there * 0.125 + 1.0) * p_now - 0.0625 * p_before
    whole = jnp.full((levels, 128), t_now, f32)
    row = lax.broadcasted_iota(jnp.int32, (levels, 128), 0)
    col = lax.broadcasted_iota(jnp.int32, (levels, 128), 1)
    apart = jnp.abs(row - col)
    decay = jnp.full((levels, 128), 0.4 * 0.125, f32)
    for b in range(6):
        decay = jnp.where((apart & (1 << b)) != 0, decay * (0.25 ** (1 << b)), decay)
    t_col, p_col = theta[...], phi[...]
    same = row == col
    t_row = jnp.sum(jnp.where(same, t_col, 0.0), axis=0, keepdims=True)
    p_row = jnp.sum(jnp.where(same, p_col, 0.0), axis=0, keepdims=True)
    inverse = (jnp.where(row <= col, t_col * p_row, p_col * t_row) * decay / whole)[:, :levels]
    inv_hi, inv_lo = halves(inverse)
    weights = jnp.concatenate([inv_hi, inv_hi, inv_lo], axis=1)

    def apply(value):
        high, low = halves(value)
        stacked = jnp.concatenate([high, low, high], axis=0)
        return jnp.dot(weights, stacked, preferred_element_type=f32)

    def area(e):
        return wide_a[nx + e - own : nx + e - own + 1, :]

    def sides(u, sides_of, e):
        n = u.shape[1]
        index = lane[:, :n]
        low = pltpu.roll(sides_of[:, :128], (125 - 8 * e) % 128, 1)
        high = pltpu.roll(sides_of[:, 128:], (123 - 8 * e) % 128, 1)
        if n == 128:
            down = jnp.where(index == 0, low, pltpu.roll(u, 1, 1))
            return down + jnp.where(index == n - 1, high, pltpu.roll(u, n - 1, 1))
        edge = jnp.concatenate([low, high], axis=1)
        down = jnp.where(index == 0, edge, pltpu.roll(u, 1, 1))
        return down + jnp.where(index == n - 1, edge, pltpu.roll(u, n - 1, 1))

    def smooth(field, sides_of, e):
        u = field[e]
        nb = field[e - 1] + field[e + 1] + sides(u, sides_of, e)
        a = area(e)
        return 0.6 * u + apply(rhs_x[e] + (4.0 - 4.0 * a) * u + a * nb)

    def smooth_strip(s, right_side, a):
        nb = pltpu.roll(s, 1, 1) + pltpu.roll(s, ny - 1, 1) + pltpu.roll(s, 8, 1) + pltpu.roll(s, ny - 8, 1)
        return 0.6 * s + apply(right_side + (4.0 - 4.0 * a) * s + a * nb)

    def horizontal(field, sides_of, e):
        u = field[e]
        nb = field[e - 1] + field[e + 1] + sides(u, sides_of, e)
        return u, rhs_x[e] - area(e) * (4.0 * u - nb)

    def vertical(v):
        above = jnp.where(level == levels - 1, 0.0, pltpu.roll(v, levels - 1, 0))
        below = jnp.where(level == 0, 0.0, pltpu.roll(v, 1, 0))
        s = jnp.concatenate([stiff_b[...]] * (ny // 128), axis=1)
        return (s + 4.0) * v - 2.0 * (above + below)

    pick = jnp.where(
        lax.broadcasted_iota(jnp.int32, (ny, cy), 0) // 2 == lax.broadcasted_iota(jnp.int32, (ny, cy), 1),
        1.0, 0.0,
    ).astype(bf16)
    spread = jnp.where(
        lax.broadcasted_iota(jnp.int32, (cy, ny), 1) // 2 == lax.broadcasted_iota(jnp.int32, (cy, ny), 0),
        1.0, 0.0,
    ).astype(bf16)
    fine_lane = lax.broadcasted_iota(jnp.int32, (128, 128), 1)
    spread_strip = jnp.where(
        lax.broadcasted_iota(jnp.int32, (128, 128), 0)
        == 8 * ((fine_lane // 8 + 3) // 2) + 2 + (fine_lane % 8) // 2,
        1.0, 0.0,
    ).astype(bf16)

    def exact(value, matrix):
        rows = value.shape[0]
        high, low = halves(value)
        both = jnp.dot(jnp.concatenate([high, low], axis=0), matrix, preferred_element_type=f32)
        return both[:rows] + both[rows:]

    for e in range(own, own + nx):
        u1[e] = apply(rhs_x[e])

    arrive("strip")
    halo = jnp.where(inner, strip[0], strip[1])
    corner_of[0, 0] = squeeze(halo, own)
    corner_of[0, 1] = squeeze(halo, own + nx - 2)
    start("corner")
    first = apply(strips(pack_rhs, halo, halo))
    for e in range(own + 1, own + nx - 1):
        u2[e] = smooth(u1, first, e)

    arrive("areas")
    eight = lane_c[:8]
    packed_a = jnp.zeros((8, 128), f32)
    for e in range(0, nx + 6):
        v = jnp.broadcast_to(area(e), (8, ny))
        v = pltpu.roll(jnp.where(eight < 4, v[:, :128], v[:, ny - 128 :]), 8 * e + 4, 1)
        packed_a = jnp.where(eight // 8 == e, v, packed_a)
    sums = []
    for x in range(-2, cx + 2):
        at = nx + 2 * x
        sums.append(jnp.broadcast_to(0.0625 * (wide_a[at : at + 1, :] + wide_a[at + 1 : at + 2, :]), (8, ny)))
    coef = exact(jnp.concatenate(sums, axis=0), pick)
    coef = {x: coef[8 * (x + 2) : 8 * (x + 2) + 8] for x in range(-2, cx + 2)}
    packed_c = jnp.zeros((8, 128), f32)
    for x in range(-2, cx + 2):
        v = pltpu.roll(coef[x], 8 * (x + 3) + 4, 1)
        packed_c = jnp.where(eight // 8 == x + 3, v, packed_c)
    pack_a[0:8, :] = packed_a
    pack_a[8:16, :] = packed_c
    start("strip_a")

    arrive("rhs")
    start("u2near")
    outer = (own - 2, own - 1, own + nx, own + nx + 1)
    for e in outer:
        u1[e] = apply(rhs_x[e])
    pack_all = packed([(e, rhs_x[e]) for e in outer], pack_rhs)
    arrive("corner", "strip_a")
    halo = jnp.where(
        row_c < own, unsqueeze(corner[0, 0], own - 2),
        jnp.where(row_c >= own + nx, unsqueeze(corner[0, 1], own + nx), halo),
    )
    rhs_strip = strips(pack_all, halo, halo)
    inner_a = eight % 8 < 4

    def strips_a(low, high, mine):
        return jnp.concatenate([jnp.where(inner_a, low, mine), jnp.where(inner_a, mine, high)], axis=1)[:1]

    a_strip = strips_a(strip_a[0, 0:8, :], strip_a[1, 0:8, :], packed_a)
    c_strip = strips_a(strip_a[0, 8:16, :], strip_a[1, 8:16, :], packed_c)
    first = apply(rhs_strip)
    for e in (own - 1, own, own + nx - 1, own + nx):
        u2[e] = smooth(u1, first, e)
    second = smooth_strip(first, rhs_strip, a_strip)

    s = stiff_b[...]
    keep = jnp.sqrt(s + 0.25 * s * s) - 0.5 * s
    r = 1.0 - keep
    power = [jnp.ones_like(r)]
    for _ in range(4 * cx + 6):
        power.append(power[-1] * r)
    is_last = w == n_w - 1
    far = jnp.ones_like(r)
    base = power[2 * cx]
    steps = jnp.maximum(n_w - 2 - w, 0)
    for b in range(len(strides)):
        far = jnp.where((steps >> b) % 2 == 1, far * base, far)
        base = base * base
    tail = jnp.where(is_last, power[0], far * power[2 * cx])
    scale = keep / (1.0 + r)

    for x in range(cx):
        e = own + 2 * x
        u_a, h_a = horizontal(u2, second, e)
        u_b, h_b = horizontal(u2, second, e + 1)
        coarse[4 + x] = exact(0.25 * (h_a + h_b - vertical(u_a + u_b)), pick)
    mine = [coarse[4 + x] for x in range(cx)]
    forward = mine[0]
    for x in range(1, cx):
        forward = mine[x] + r * forward
    backward = sum((power[x] - tail * power[2 * cx - x]) * mine[x] for x in range(cx))
    enter = jnp.zeros_like(forward)
    leave = jnp.zeros_like(forward)
    step_all = power[cx]
    step_less = None
    scans = []
    for i, s in enumerate(strides):
        scan_f[i] = forward
        scan_z[i] = backward
        right = pltpu.make_async_remote_copy(
            src_ref=scan_f.at[i], dst_ref=scan_rf.at[i], send_sem=scan_send.at[i, 0], recv_sem=scan_recv.at[i, 0],
            device_id={"wide": jnp.minimum(w + s, n_w - 1)}, device_id_type=MESH,
        )
        left = pltpu.make_async_remote_copy(
            src_ref=scan_z.at[i], dst_ref=scan_rz.at[i], send_sem=scan_send.at[i, 1], recv_sem=scan_recv.at[i, 1],
            device_id={"wide": jnp.maximum(w - s, 0)}, device_id_type=MESH,
        )
        scans.append((right, left, s))

        @pl.when(w < n_w - s)
        def _():
            right.start()

        @pl.when(w >= s)
        def _():
            left.start()

        if i == 0:
            start("coarse")
            start("u2far")
            halo = jnp.where(inner, second[:, :128], second[:, 128:])
            corner_of[1, 0] = squeeze(halo, own + 1)
            corner_of[1, 1] = squeeze(halo, own + nx - 3)
            start("u2corner")

        @pl.when(w >= s)
        def _():
            right.wait_recv()

        @pl.when(w < n_w - s)
        def _():
            left.wait_recv()

        got_f, got_z = scan_rf[i], scan_rz[i]
        forward = forward + step_all * got_f
        backward = backward + step_all * got_z
        enter = enter + (step_less * got_f if i else got_f)
        leave = leave + (step_less * got_z if i else got_z)
        step_less = step_less * step_all if i else step_all
        step_all = step_all * step_all

    arrive("coarse")
    inverse_r = 1.0 / r
    image = {
        t: 1.0 - jnp.where(is_last, power[max(2 * cx - 2 * t, 0)], far * power[4 * cx - 2 * t])
        for t in range(-3, cx + 3)
    }
    before = {-1: enter}
    for t in range(cx + 2):
        before[t] = coarse[4 + t] + r * before[t - 1]
    for t in (-2, -3):
        before[t] = (before[t + 1] - coarse[4 + t + 1]) * inverse_r
    after = {cx: leave}
    for t in reversed(range(-2, cx)):
        after[t] = image[t] * coarse[4 + t] + r * after[t + 1]
    for t in (cx + 1, cx + 2):
        after[t] = (after[t - 1] - image[t - 1] * coarse[4 + t - 1]) * inverse_r
    for t in range(-3, cx + 3):
        if t < cx:
            value = scale * (image[t] * before[t] + r * after[t + 1])
        else:
            value = scale * (image[t] * r * before[t - 1] + after[t])
        if t < 0:
            value = jnp.where(w == 0, 0.0, value)
        if t >= cx:
            value = jnp.where(is_last, 0.0, value)
        line[4 + t] = value
    pack_c = packed([(t + 3, coarse[4 + t]) for t in range(-2, cx + 2)])
    pack_l = packed([(t + 3, line[4 + t]) for t in range(-3, cx + 3)])
    pack[1] = pack_c
    pack[2] = pack_l
    start("line")

    arrive("u2near", "u2far", "u2corner")
    halo = jnp.where(
        row_c < own - 1, unsqueeze(corner[1, 0], own - 3),
        jnp.where(row_c > own + nx, unsqueeze(corner[1, 1], own + nx + 1), halo),
    )
    second = strips(packed([(e, u2[e]) for e in range(nx + 6)]), halo, halo)

    arrive("line")
    c_sides = strips(pack_c, strip[2], strip[4])
    l_sides = strips(pack_l, strip[3], strip[5])

    def correction(x):
        v = line[4 + x]
        nb = line[3 + x] + line[5 + x] + sides(v, l_sides, x + 3)
        a = coef[x][:1]
        return exact(0.6 * v + apply(coarse[4 + x] + (4.0 - 4.0 * a) * v + a * nb), spread)

    for x in range(-2, cx + 2):
        value = correction(x)
        for e in (own + 2 * x, own + 2 * x + 1):
            if 0 <= e < nx + 6:
                u3[e] = u2[e] + value
    fix = smooth_strip(l_sides, c_sides, c_strip)
    fix = exact(jnp.concatenate([fix[:, :128], fix[:, 128:]], axis=0), spread_strip)
    third = second + jnp.concatenate([fix[:levels], fix[levels:]], axis=1)
    for e in range(1, nx + 5):
        u4[e] = smooth(u3, third, e)
    fourth = smooth_strip(third, rhs_strip, a_strip)
    for e in range(2, nx + 4):
        p[e] = smooth(u4, fourth, e)
    fifth = smooth_strip(fourth, rhs_strip, a_strip)
    for x in range(nx):
        u, h = horizontal(p, fifth, own + x)
        left_over = h - vertical(u)
        for t in range(tiles):
            at = pl.ds(x + nx * t, levels, stride=tiles * nx)
            p_out[at, :] = u[:, 128 * t : 128 * t + 128]
            r_out[at, :] = left_over[:, 128 * t : 128 * t + 128]

    for name in names:
        for copy, goes, _ in copies(name):
            @pl.when(goes)
            def _():
                copy.wait_send()
    for right, left, s in scans:
        @pl.when(w < n_w - s)
        def _():
            right.wait_send()

        @pl.when(w >= s)
        def _():
            left.wait_send()


def local(n_w, n_n, rhs, areas, stiffness):
    levels, nx, ny = rhs.shape
    cx, tiles = nx // 2, ny // 128
    steps = max(1, (n_w - 1).bit_length())
    vmem = lambda *shape: pltpu.VMEM(shape, f32)
    whole = pl.BlockSpec(memory_space=pltpu.VMEM)
    outs = pl.pallas_call(
        functools.partial(kernel, n_w, n_n, nx, ny, levels),
        out_shape=[jax.ShapeDtypeStruct((levels * nx * tiles, 128), f32)] * 2,
        in_specs=[whole, whole, pl.BlockSpec(memory_space=pltpu.SMEM)],
        out_specs=[whole, whole],
        scratch_shapes=[vmem(nx + 6, levels, ny)] * 6
        + [
            vmem(3 * nx, ny), vmem(cx + 8, levels, 128), vmem(cx + 8, levels, 128),
            vmem(3, levels, 128), vmem(6, levels, 128), vmem(2, 2, 8, 128), vmem(2, 2, 8, 128),
            vmem(16, 128), vmem(2, 16, 128),
            vmem(steps, levels, 128), vmem(steps, levels, 128),
            vmem(steps, levels, 128), vmem(steps, levels, 128),
            vmem(levels, 128), vmem(levels, 128), vmem(levels, 128),
            pltpu.SemaphoreType.DMA((10, 2)), pltpu.SemaphoreType.DMA((10, 2)),
            pltpu.SemaphoreType.DMA((steps, 2)), pltpu.SemaphoreType.DMA((steps, 2)),
        ],
        compiler_params=pltpu.CompilerParams(
            collective_id=0, has_side_effects=True, vmem_limit_bytes=40 * 1024 * 1024
        ),
        cost_estimate=pl.CostEstimate(flops=80_000_000, bytes_accessed=1_600_000, transcendentals=0),
    )(rhs.reshape(levels, nx, tiles, 128).transpose(0, 2, 1, 3).reshape(-1, 128), areas, stiffness)
    return tuple(v.reshape(levels, tiles, nx, 128).transpose(0, 2, 1, 3).reshape(rhs.shape) for v in outs)


def solution(mesh):
    placed = (P(None, "wide", "narrow"), P("wide", "narrow"), P())
    return jax.shard_map(
        functools.partial(local, mesh.shape["wide"], mesh.shape["narrow"]),
        mesh=mesh,
        in_specs=placed,
        out_specs=(P(None, "wide", "narrow"), P(None, "wide", "narrow")),
        check_vma=False,
    )
```

```python
import functools

import jax
import jax.numpy as jnp
from jax import lax
from jax.experimental import pallas as pl
from jax.experimental.pallas import tpu as pltpu
from jax.sharding import PartitionSpec as P

MESH = pl.DeviceIdType.MESH
f32 = jnp.float32
bf16 = jnp.bfloat16


def halves(value):
    high = value.astype(bf16)
    return high, (value - high.astype(f32)).astype(bf16)


def kernel(
    n_w, n_n, nx, ny, levels,
    rhs_in, areas_in, stiff_in, p_out, r_out,
    rhs_ref, stiff_ref, in_sem,
    rhs_x, u1, u2, u3, u4, p, wide_a, coarse, line, pack, strip, corner_of, corner, pack_a, strip_a,
    scan_f, scan_z, scan_rf, scan_rz, theta, phi, stiff_b,
    send_sem, recv_sem, scan_send, scan_recv,
):
    cx, cy = nx // 2, ny // 2
    w, c = lax.axis_index("wide"), lax.axis_index("narrow")
    has = (w > 0, w < n_w - 1, c > 0, c < n_n - 1)
    to = (
        {"wide": jnp.maximum(w - 1, 0)},
        {"wide": jnp.minimum(w + 1, n_w - 1)},
        {"narrow": jnp.maximum(c - 1, 0)},
        {"narrow": jnp.minimum(c + 1, n_n - 1)},
    )
    strides = []
    while (1 << len(strides)) < n_w:
        strides.append(1 << len(strides))
    own = 3
    tiles = ny // 128

    inputs = [
        pltpu.make_async_copy(rhs_in, rhs_ref, in_sem.at[0]),
        pltpu.make_async_copy(stiff_in, stiff_ref, in_sem.at[1]),
        pltpu.make_async_copy(areas_in, wide_a.at[pl.ds(nx, nx)], in_sem.at[2]),
    ]
    for copy in inputs:
        copy.start()

    small = jnp.zeros((levels, 128), f32)
    nothing = jnp.zeros((levels, ny), f32)
    edge_x = (
        ((1, 2), (0, 1), (2, 3)),
        ((nx + 3, nx + 4), (nx + 4, nx + 5), (cx + 4, cx + 5)),
    )
    rhs_x[0] = nothing
    rhs_x[nx + 5] = nothing
    for side in range(2):
        @pl.when(jnp.logical_not(has[side]))
        def _():
            for e in edge_x[side][0]:
                rhs_x[e] = nothing
            for e in edge_x[side][1]:
                u2[e] = nothing
            for e in edge_x[side][2]:
                coarse[e] = small
            corner[0, side] = small[:8]
            corner[1, side] = small[:8]
            wide_a[2 * side * nx : 2 * side * nx + nx, :] = jnp.zeros((nx, ny), f32)

        @pl.when(jnp.logical_not(has[2 + side]))
        def _():
            strip[side] = small
            strip[2 + 2 * side] = small
            strip[3 + 2 * side] = small
            strip_a[side] = jnp.zeros((16, 128), f32)
    for i, s in enumerate(strides):
        @pl.when(w < s)
        def _():
            scan_rf[i] = small

        @pl.when(w >= n_w - s)
        def _():
            scan_rz[i] = small

    barrier = pltpu.get_barrier_semaphore()
    for side in range(4):
        @pl.when(has[side])
        def _():
            pl.semaphore_signal(barrier, inc=1, device_id=to[side], device_id_type=MESH)
    for s in strides[1:]:
        @pl.when(w >= s)
        def _():
            pl.semaphore_signal(
                barrier, inc=1, device_id={"wide": jnp.maximum(w - s, 0)}, device_id_type=MESH
            )

        @pl.when(w < n_w - s)
        def _():
            pl.semaphore_signal(
                barrier, inc=1, device_id={"wide": jnp.minimum(w + s, n_w - 1)}, device_id_type=MESH
            )

    exchanges = {
        "areas": (0, (wide_a.at[pl.ds(nx, nx)], wide_a.at[pl.ds(2 * nx, nx)]),
                  (wide_a.at[pl.ds(nx, nx)], wide_a.at[pl.ds(0, nx)])),
        "rhs": (0, (rhs_x.at[pl.ds(own, 2)], rhs_x.at[pl.ds(own + nx, 2)]),
                (rhs_x.at[pl.ds(own + nx - 2, 2)], rhs_x.at[pl.ds(own - 2, 2)])),
        "corner": (0, (corner_of.at[0, 0], corner.at[0, 1]), (corner_of.at[0, 1], corner.at[0, 0])),
        "u2near": (0, (u2.at[own + 1], u2.at[own + nx + 1]), (u2.at[own + nx - 2], u2.at[own - 2])),
        "u2far": (0, (u2.at[own + 2], u2.at[own + nx + 2]), (u2.at[own + nx - 3], u2.at[own - 3])),
        "u2corner": (0, (corner_of.at[1, 0], corner.at[1, 1]), (corner_of.at[1, 1], corner.at[1, 0])),
        "coarse": (0, (coarse.at[pl.ds(4, 2)], coarse.at[pl.ds(4 + cx, 2)]),
                   (coarse.at[pl.ds(2 + cx, 2)], coarse.at[pl.ds(2, 2)])),
        "strip": (1, (pack.at[0], strip.at[1]), (pack.at[0], strip.at[0])),
        "strip_a": (1, (pack_a, strip_a.at[1]), (pack_a, strip_a.at[0])),
        "line": (1, (pack.at[pl.ds(1, 2)], strip.at[pl.ds(4, 2)]), (pack.at[pl.ds(1, 2)], strip.at[pl.ds(2, 2)])),
    }
    names = list(exchanges)

    def copies(name):
        axis, low, high = exchanges[name]
        at = names.index(name)
        return [
            (
                pltpu.make_async_remote_copy(
                    src_ref=pair[0], dst_ref=pair[1], send_sem=send_sem.at[at, i], recv_sem=recv_sem.at[at, i],
                    device_id=to[2 * axis + i], device_id_type=MESH,
                ),
                has[2 * axis + i],
                has[2 * axis + 1 - i],
            )
            for i, pair in enumerate((low, high))
        ]

    def start(name):
        for copy, goes, _ in copies(name):
            @pl.when(goes)
            def _():
                copy.start()

    def arrive(*which):
        for name in which:
            for copy, _, comes in copies(name):
                @pl.when(comes)
                def _():
                    copy.wait_recv()

    lane = lax.broadcasted_iota(jnp.int32, (levels, ny), 1)
    lane_c = lax.broadcasted_iota(jnp.int32, (levels, 128), 1)
    level = lax.broadcasted_iota(jnp.int32, (levels, ny), 0)
    inner = lane_c % 8 < 4
    row_c = lane_c // 8

    def packed(rows, base=None):
        result = jnp.zeros((levels, 128), f32) if base is None else base
        for e, value in rows:
            ends = jnp.where(lane_c < 4, value[:, :128], value[:, value.shape[1] - 128 :])
            result = jnp.where(row_c == e, pltpu.roll(ends, 8 * e + 4, 1), result)
        return result

    def strips(mine, low, high):
        return jnp.concatenate([jnp.where(inner, low, mine), jnp.where(inner, mine, high)], axis=1)

    def squeeze(tile, e):
        result = jnp.zeros((8, 128), f32)
        for b in range(levels // 8):
            part = pltpu.roll(tile[8 * b : 8 * b + 8], (16 * b - 8 * e) % 128, 1)
            result = jnp.where(lane_c[:8] // 16 == b, part, result)
        return result

    def unsqueeze(tile, e):
        return jnp.concatenate([pltpu.roll(tile, (8 * e - 16 * b) % 128, 1) for b in range(levels // 8)], axis=0)

    inputs[0].wait()
    for x in (0, 1, nx - 2, nx - 1) + tuple(range(2, nx - 2)):
        rhs_x[own + x] = jnp.concatenate(
            [rhs_ref[pl.ds(x + nx * t, levels, stride=tiles * nx), :] for t in range(tiles)], axis=1
        )
    peers = sum(h.astype(jnp.int32) for h in has)
    for s in strides[1:]:
        peers = peers + (w >= s).astype(jnp.int32) + (w < n_w - s).astype(jnp.int32)
    pl.semaphore_wait(barrier, peers)
    inputs[2].wait()
    start("areas")
    start("rhs")
    pack_rhs = packed([(e, rhs_x[e]) for e in range(own, own + nx)])
    pack[0] = pack_rhs
    start("strip")

    inputs[1].wait()
    zero, one = jnp.float32(0.0), jnp.float32(1.0)
    t_before, t_now, p_before, p_now = zero, one, zero, one
    for i in range(levels):
        j = levels - 1 - i
        here, there = stiff_ref[i], stiff_ref[j]
        theta[i : i + 1, :] = jnp.full((1, 128), t_now, f32)
        phi[j : j + 1, :] = jnp.full((1, 128), p_now, f32)
        stiff_b[i : i + 1, :] = jnp.full((1, 128), here, f32)
        t_before, t_now = t_now, (here * 0.125 + 1.0) * t_now - 0.0625 * t_before
        p_before, p_now = p_now, (there * 0.125 + 1.0) * p_now - 0.0625 * p_before
    whole = jnp.full((levels, 128), t_now, f32)
    row = lax.broadcasted_iota(jnp.int32, (levels, 128), 0)
    col = lax.broadcasted_iota(jnp.int32, (levels, 128), 1)
    apart = jnp.abs(row - col)
    decay = jnp.full((levels, 128), 0.4 * 0.125, f32)
    for b in range(6):
        decay = jnp.where((apart & (1 << b)) != 0, decay * (0.25 ** (1 << b)), decay)
    t_col, p_col = theta[...], phi[...]
    same = row == col
    t_row = jnp.sum(jnp.where(same, t_col, 0.0), axis=0, keepdims=True)
    p_row = jnp.sum(jnp.where(same, p_col, 0.0), axis=0, keepdims=True)
    inverse = (jnp.where(row <= col, t_col * p_row, p_col * t_row) * decay / whole)[:, :levels]
    inv_hi, inv_lo = halves(inverse)
    weights = jnp.concatenate([inv_hi, inv_hi, inv_lo], axis=1)

    def apply(value):
        high, low = halves(value)
        stacked = jnp.concatenate([high, low, high], axis=0)
        return jnp.dot(weights, stacked, preferred_element_type=f32)

    def area(e):
        return wide_a[nx + e - own : nx + e - own + 1, :]

    def sides(u, sides_of, e):
        n = u.shape[1]
        index = lane[:, :n]
        low = pltpu.roll(sides_of[:, :128], (125 - 8 * e) % 128, 1)
        high = pltpu.roll(sides_of[:, 128:], (123 - 8 * e) % 128, 1)
        if n == 128:
            down = jnp.where(index == 0, low, pltpu.roll(u, 1, 1))
            return down + jnp.where(index == n - 1, high, pltpu.roll(u, n - 1, 1))
        edge = jnp.concatenate([low, high], axis=1)
        down = jnp.where(index == 0, edge, pltpu.roll(u, 1, 1))
        return down + jnp.where(index == n - 1, edge, pltpu.roll(u, n - 1, 1))

    def smooth(field, sides_of, e):
        u = field[e]
        nb = field[e - 1] + field[e + 1] + sides(u, sides_of, e)
        a = area(e)
        return 0.6 * u + apply(rhs_x[e] + (4.0 - 4.0 * a) * u + a * nb)

    def smooth_strip(s, right_side, a):
        nb = pltpu.roll(s, 1, 1) + pltpu.roll(s, ny - 1, 1) + pltpu.roll(s, 8, 1) + pltpu.roll(s, ny - 8, 1)
        return 0.6 * s + apply(right_side + (4.0 - 4.0 * a) * s + a * nb)

    def horizontal(field, sides_of, e):
        u = field[e]
        nb = field[e - 1] + field[e + 1] + sides(u, sides_of, e)
        return u, rhs_x[e] - area(e) * (4.0 * u - nb)

    def vertical(v):
        above = jnp.where(level == levels - 1, 0.0, pltpu.roll(v, levels - 1, 0))
        below = jnp.where(level == 0, 0.0, pltpu.roll(v, 1, 0))
        s = jnp.concatenate([stiff_b[...]] * (ny // 128), axis=1)
        return (s + 4.0) * v - 2.0 * (above + below)

    pick = jnp.where(
        lax.broadcasted_iota(jnp.int32, (ny, cy), 0) // 2 == lax.broadcasted_iota(jnp.int32, (ny, cy), 1),
        1.0, 0.0,
    ).astype(bf16)
    spread = jnp.where(
        lax.broadcasted_iota(jnp.int32, (cy, ny), 1) // 2 == lax.broadcasted_iota(jnp.int32, (cy, ny), 0),
        1.0, 0.0,
    ).astype(bf16)
    fine_lane = lax.broadcasted_iota(jnp.int32, (128, 128), 1)
    spread_strip = jnp.where(
        lax.broadcasted_iota(jnp.int32, (128, 128), 0)
        == 8 * ((fine_lane // 8 + 3) // 2) + 2 + (fine_lane % 8) // 2,
        1.0, 0.0,
    ).astype(bf16)

    def exact(value, matrix):
        rows = value.shape[0]
        high, low = halves(value)
        both = jnp.dot(jnp.concatenate([high, low], axis=0), matrix, preferred_element_type=f32)
        return both[:rows] + both[rows:]

    for e in range(own, own + nx):
        u1[e] = apply(rhs_x[e])

    arrive("strip")
    halo = jnp.where(inner, strip[0], strip[1])
    corner_of[0, 0] = squeeze(halo, own)
    corner_of[0, 1] = squeeze(halo, own + nx - 2)
    start("corner")
    first = apply(strips(pack_rhs, halo, halo))
    for e in range(own + 1, own + nx - 1):
        u2[e] = smooth(u1, first, e)

    arrive("areas")
    eight = lane_c[:8]
    packed_a = jnp.zeros((8, 128), f32)
    for e in range(0, nx + 6):
        v = jnp.broadcast_to(area(e), (8, ny))
        v = pltpu.roll(jnp.where(eight < 4, v[:, :128], v[:, ny - 128 :]), 8 * e + 4, 1)
        packed_a = jnp.where(eight // 8 == e, v, packed_a)
    sums = []
    for x in range(-2, cx + 2):
        at = nx + 2 * x
        sums.append(jnp.broadcast_to(0.0625 * (wide_a[at : at + 1, :] + wide_a[at + 1 : at + 2, :]), (8, ny)))
    coef = exact(jnp.concatenate(sums, axis=0), pick)
    coef = {x: coef[8 * (x + 2) : 8 * (x + 2) + 8] for x in range(-2, cx + 2)}
    packed_c = jnp.zeros((8, 128), f32)
    for x in range(-2, cx + 2):
        v = pltpu.roll(coef[x], 8 * (x + 3) + 4, 1)
        packed_c = jnp.where(eight // 8 == x + 3, v, packed_c)
    pack_a[0:8, :] = packed_a
    pack_a[8:16, :] = packed_c
    start("strip_a")

    arrive("rhs")
    start("u2near")
    outer = (own - 2, own - 1, own + nx, own + nx + 1)
    for e in outer:
        u1[e] = apply(rhs_x[e])
    pack_all = packed([(e, rhs_x[e]) for e in outer], pack_rhs)
    arrive("corner", "strip_a")
    halo = jnp.where(
        row_c < own, unsqueeze(corner[0, 0], own - 2),
        jnp.where(row_c >= own + nx, unsqueeze(corner[0, 1], own + nx), halo),
    )
    rhs_strip = strips(pack_all, halo, halo)
    inner_a = eight % 8 < 4

    def strips_a(low, high, mine):
        return jnp.concatenate([jnp.where(inner_a, low, mine), jnp.where(inner_a, mine, high)], axis=1)[:1]

    a_strip = strips_a(strip_a[0, 0:8, :], strip_a[1, 0:8, :], packed_a)
    c_strip = strips_a(strip_a[0, 8:16, :], strip_a[1, 8:16, :], packed_c)
    first = apply(rhs_strip)
    for e in (own - 1, own, own + nx - 1, own + nx):
        u2[e] = smooth(u1, first, e)
    second = smooth_strip(first, rhs_strip, a_strip)

    s = stiff_b[...]
    keep = jnp.sqrt(s + 0.25 * s * s) - 0.5 * s
    r = 1.0 - keep
    power = [jnp.ones_like(r)]
    for _ in range(4 * cx + 6):
        power.append(power[-1] * r)
    is_last = w == n_w - 1
    far = jnp.ones_like(r)
    base = power[2 * cx]
    steps = jnp.maximum(n_w - 2 - w, 0)
    for b in range(len(strides)):
        far = jnp.where((steps >> b) % 2 == 1, far * base, far)
        base = base * base
    tail = jnp.where(is_last, power[0], far * power[2 * cx])
    scale = keep / (1.0 + r)

    for x in range(cx):
        e = own + 2 * x
        u_a, h_a = horizontal(u2, second, e)
        u_b, h_b = horizontal(u2, second, e + 1)
        coarse[4 + x] = exact(0.25 * (h_a + h_b - vertical(u_a + u_b)), pick)
    mine = [coarse[4 + x] for x in range(cx)]
    forward = mine[0]
    for x in range(1, cx):
        forward = mine[x] + r * forward
    backward = sum((power[x] - tail * power[2 * cx - x]) * mine[x] for x in range(cx))
    enter = jnp.zeros_like(forward)
    leave = jnp.zeros_like(forward)
    step_all = power[cx]
    step_less = None
    scans = []
    for i, s in enumerate(strides):
        scan_f[i] = forward
        scan_z[i] = backward
        right = pltpu.make_async_remote_copy(
            src_ref=scan_f.at[i], dst_ref=scan_rf.at[i], send_sem=scan_send.at[i, 0], recv_sem=scan_recv.at[i, 0],
            device_id={"wide": jnp.minimum(w + s, n_w - 1)}, device_id_type=MESH,
        )
        left = pltpu.make_async_remote_copy(
            src_ref=scan_z.at[i], dst_ref=scan_rz.at[i], send_sem=scan_send.at[i, 1], recv_sem=scan_recv.at[i, 1],
            device_id={"wide": jnp.maximum(w - s, 0)}, device_id_type=MESH,
        )
        scans.append((right, left, s))

        @pl.when(w < n_w - s)
        def _():
            right.start()

        @pl.when(w >= s)
        def _():
            left.start()

        if i == 0:
            start("coarse")
            start("u2far")
            halo = jnp.where(inner, second[:, :128], second[:, 128:])
            corner_of[1, 0] = squeeze(halo, own + 1)
            corner_of[1, 1] = squeeze(halo, own + nx - 3)
            start("u2corner")

        @pl.when(w >= s)
        def _():
            right.wait_recv()

        @pl.when(w < n_w - s)
        def _():
            left.wait_recv()

        got_f, got_z = scan_rf[i], scan_rz[i]
        forward = forward + step_all * got_f
        backward = backward + step_all * got_z
        enter = enter + (step_less * got_f if i else got_f)
        leave = leave + (step_less * got_z if i else got_z)
        step_less = step_less * step_all if i else step_all
        step_all = step_all * step_all

    arrive("coarse")
    inverse_r = 1.0 / r
    image = {
        t: 1.0 - jnp.where(is_last, power[max(2 * cx - 2 * t, 0)], far * power[4 * cx - 2 * t])
        for t in range(-3, cx + 3)
    }
    before = {-1: enter}
    for t in range(cx + 2):
        before[t] = coarse[4 + t] + r * before[t - 1]
    for t in (-2, -3):
        before[t] = (before[t + 1] - coarse[4 + t + 1]) * inverse_r
    after = {cx: leave}
    for t in reversed(range(-2, cx)):
        after[t] = image[t] * coarse[4 + t] + r * after[t + 1]
    for t in (cx + 1, cx + 2):
        after[t] = (after[t - 1] - image[t - 1] * coarse[4 + t - 1]) * inverse_r
    for t in range(-3, cx + 3):
        if t < cx:
            value = scale * (image[t] * before[t] + r * after[t + 1])
        else:
            value = scale * (image[t] * r * before[t - 1] + after[t])
        if t < 0:
            value = jnp.where(w == 0, 0.0, value)
        if t >= cx:
            value = jnp.where(is_last, 0.0, value)
        line[4 + t] = value
    pack_c = packed([(t + 3, coarse[4 + t]) for t in range(-2, cx + 2)])
    pack_l = packed([(t + 3, line[4 + t]) for t in range(-3, cx + 3)])
    pack[1] = pack_c
    pack[2] = pack_l
    start("line")

    arrive("u2near", "u2far", "u2corner")
    halo = jnp.where(
        row_c < own - 1, unsqueeze(corner[1, 0], own - 3),
        jnp.where(row_c > own + nx, unsqueeze(corner[1, 1], own + nx + 1), halo),
    )
    second = strips(packed([(e, u2[e]) for e in range(nx + 6)]), halo, halo)

    arrive("line")
    c_sides = strips(pack_c, strip[2], strip[4])
    l_sides = strips(pack_l, strip[3], strip[5])

    def correction(x):
        v = line[4 + x]
        nb = line[3 + x] + line[5 + x] + sides(v, l_sides, x + 3)
        a = coef[x][:1]
        return exact(0.6 * v + apply(coarse[4 + x] + (4.0 - 4.0 * a) * v + a * nb), spread)

    for x in range(-2, cx + 2):
        value = correction(x)
        for e in (own + 2 * x, own + 2 * x + 1):
            if 0 <= e < nx + 6:
                u3[e] = u2[e] + value
    fix = smooth_strip(l_sides, c_sides, c_strip)
    fix = exact(jnp.concatenate([fix[:, :128], fix[:, 128:]], axis=0), spread_strip)
    third = second + jnp.concatenate([fix[:levels], fix[levels:]], axis=1)
    for e in range(1, nx + 5):
        u4[e] = smooth(u3, third, e)
    fourth = smooth_strip(third, rhs_strip, a_strip)
    for e in range(2, nx + 4):
        p[e] = smooth(u4, fourth, e)
    fifth = smooth_strip(fourth, rhs_strip, a_strip)
    for x in range(nx):
        u, h = horizontal(p, fifth, own + x)
        left_over = h - vertical(u)
        for t in range(tiles):
            at = pl.ds(x + nx * t, levels, stride=tiles * nx)
            p_out[at, :] = u[:, 128 * t : 128 * t + 128]
            r_out[at, :] = left_over[:, 128 * t : 128 * t + 128]

    for name in names:
        for copy, goes, _ in copies(name):
            @pl.when(goes)
            def _():
                copy.wait_send()
    for right, left, s in scans:
        @pl.when(w < n_w - s)
        def _():
            right.wait_send()

        @pl.when(w >= s)
        def _():
            left.wait_send()


def write(p_in, r_in, p_out, r_out, sem):
    rows = p_in.shape[0] // 4
    parts = [
        pltpu.make_async_copy(
            pair[0].at[pl.ds(rows * i, rows)], pair[1].at[pl.ds(rows * i, rows)], sem.at[4 * j + i]
        )
        for j, pair in enumerate(((p_in, p_out), (r_in, r_out)))
        for i in range(4)
    ]
    for part in parts:
        part.start()
    for part in parts:
        part.wait()


def local(n_w, n_n, rhs, areas, stiffness):
    levels, nx, ny = rhs.shape
    cx, tiles = nx // 2, ny // 128
    steps = max(1, (n_w - 1).bit_length())
    vmem = lambda *shape: pltpu.VMEM(shape, f32)
    whole = pl.BlockSpec(memory_space=pltpu.VMEM)
    outs = pl.pallas_call(
        functools.partial(kernel, n_w, n_n, nx, ny, levels),
        out_shape=[jax.ShapeDtypeStruct((levels * nx * tiles, 128), f32)] * 2,
        in_specs=[pl.BlockSpec(memory_space=pltpu.HBM)] * 3,
        out_specs=[whole, whole],
        scratch_shapes=[
            vmem(levels * nx * tiles, 128), pltpu.SMEM((levels,), f32), pltpu.SemaphoreType.DMA((3,)),
        ]
        + [vmem(nx + 6, levels, ny)] * 6
        + [
            vmem(3 * nx, ny), vmem(cx + 8, levels, 128), vmem(cx + 8, levels, 128),
            vmem(3, levels, 128), vmem(6, levels, 128), vmem(2, 2, 8, 128), vmem(2, 2, 8, 128),
            vmem(16, 128), vmem(2, 16, 128),
            vmem(steps, levels, 128), vmem(steps, levels, 128),
            vmem(steps, levels, 128), vmem(steps, levels, 128),
            vmem(levels, 128), vmem(levels, 128), vmem(levels, 128),
            pltpu.SemaphoreType.DMA((10, 2)), pltpu.SemaphoreType.DMA((10, 2)),
            pltpu.SemaphoreType.DMA((steps, 2)), pltpu.SemaphoreType.DMA((steps, 2)),
        ],
        compiler_params=pltpu.CompilerParams(
            collective_id=0, has_side_effects=True, vmem_limit_bytes=56 * 1024 * 1024
        ),
        cost_estimate=pl.CostEstimate(flops=80_000_000, bytes_accessed=1_600_000, transcendentals=0),
    )(rhs.reshape(levels, nx, tiles, 128).transpose(0, 2, 1, 3).reshape(-1, 128), areas, stiffness)
    outs = pl.pallas_call(
        write,
        out_shape=[jax.ShapeDtypeStruct((levels * nx * tiles, 128), f32)] * 2,
        in_specs=[pl.BlockSpec(memory_space=pl.ANY)] * 2,
        out_specs=[pl.BlockSpec(memory_space=pl.ANY)] * 2,
        scratch_shapes=[pltpu.SemaphoreType.DMA((8,))],
        compiler_params=pltpu.CompilerParams(vmem_limit_bytes=60 * 1024 * 1024),
    )(*outs)
    return tuple(v.reshape(levels, tiles, nx, 128).transpose(0, 2, 1, 3).reshape(rhs.shape) for v in outs)


def solution(mesh):
    placed = (P(None, "wide", "narrow"), P("wide", "narrow"), P())
    return jax.shard_map(
        functools.partial(local, mesh.shape["wide"], mesh.shape["narrow"]),
        mesh=mesh,
        in_specs=placed,
        out_specs=(P(None, "wide", "narrow"), P(None, "wide", "narrow")),
        check_vma=False,
    )
```

```python
import functools

import jax
import jax.numpy as jnp
from jax import lax
from jax.experimental import pallas as pl
from jax.experimental.pallas import tpu as pltpu
from jax.sharding import PartitionSpec as P

MESH = pl.DeviceIdType.MESH
f32 = jnp.float32
bf16 = jnp.bfloat16


def halves(value):
    high = value.astype(bf16)
    return high, (value - high.astype(f32)).astype(bf16)


def kernel(
    n_w, n_n, nx, ny, levels,
    rhs_in, areas_in, stiff_in, p_out, r_out,
    rhs_ref, stiff_ref, in_sem,
    rhs_x, u1, u2, u3, u4, p, wide_a, coarse, line, pack, strip, corner_of, corner, pack_a, strip_a,
    scan_f, scan_z, scan_rf, scan_rz, theta, phi, stiff_b,
    send_sem, recv_sem, scan_send, scan_recv,
):
    cx, cy = nx // 2, ny // 2
    w, c = lax.axis_index("wide"), lax.axis_index("narrow")
    has = (w > 0, w < n_w - 1, c > 0, c < n_n - 1)
    to = (
        {"wide": jnp.maximum(w - 1, 0)},
        {"wide": jnp.minimum(w + 1, n_w - 1)},
        {"narrow": jnp.maximum(c - 1, 0)},
        {"narrow": jnp.minimum(c + 1, n_n - 1)},
    )
    strides = []
    while (1 << len(strides)) < n_w:
        strides.append(1 << len(strides))
    own = 3
    tiles = ny // 128

    inputs = [
        pltpu.make_async_copy(rhs_in, rhs_ref, in_sem.at[0]),
        pltpu.make_async_copy(stiff_in, stiff_ref, in_sem.at[1]),
        pltpu.make_async_copy(areas_in, wide_a.at[pl.ds(nx, nx)], in_sem.at[2]),
    ]
    for copy in inputs:
        copy.start()

    small = jnp.zeros((levels, 128), f32)
    nothing = jnp.zeros((levels, ny), f32)
    edge_x = (
        ((1, 2), (0, 1), (2, 3)),
        ((nx + 3, nx + 4), (nx + 4, nx + 5), (cx + 4, cx + 5)),
    )
    rhs_x[0] = nothing
    rhs_x[nx + 5] = nothing
    for side in range(2):
        @pl.when(jnp.logical_not(has[side]))
        def _():
            for e in edge_x[side][0]:
                rhs_x[e] = nothing
            for e in edge_x[side][1]:
                u2[e] = nothing
            for e in edge_x[side][2]:
                coarse[e] = small
            corner[0, side] = small[:8]
            corner[1, side] = small[:8]
            wide_a[2 * side * nx : 2 * side * nx + nx, :] = jnp.zeros((nx, ny), f32)

        @pl.when(jnp.logical_not(has[2 + side]))
        def _():
            strip[side] = small
            strip[2 + 2 * side] = small
            strip[3 + 2 * side] = small
            strip_a[side] = jnp.zeros((16, 128), f32)
    for i, s in enumerate(strides):
        @pl.when(w < s)
        def _():
            scan_rf[i] = small

        @pl.when(w >= n_w - s)
        def _():
            scan_rz[i] = small

    barrier = pltpu.get_barrier_semaphore()
    for side in range(4):
        @pl.when(has[side])
        def _():
            pl.semaphore_signal(barrier, inc=1, device_id=to[side], device_id_type=MESH)
    for s in strides[1:]:
        @pl.when(w >= s)
        def _():
            pl.semaphore_signal(
                barrier, inc=1, device_id={"wide": jnp.maximum(w - s, 0)}, device_id_type=MESH
            )

        @pl.when(w < n_w - s)
        def _():
            pl.semaphore_signal(
                barrier, inc=1, device_id={"wide": jnp.minimum(w + s, n_w - 1)}, device_id_type=MESH
            )

    exchanges = {
        "areas": (0, (wide_a.at[pl.ds(nx, nx)], wide_a.at[pl.ds(2 * nx, nx)]),
                  (wide_a.at[pl.ds(nx, nx)], wide_a.at[pl.ds(0, nx)])),
        "rhs": (0, (rhs_x.at[pl.ds(own, 2)], rhs_x.at[pl.ds(own + nx, 2)]),
                (rhs_x.at[pl.ds(own + nx - 2, 2)], rhs_x.at[pl.ds(own - 2, 2)])),
        "corner": (0, (corner_of.at[0, 0], corner.at[0, 1]), (corner_of.at[0, 1], corner.at[0, 0])),
        "u2near": (0, (u2.at[own + 1], u2.at[own + nx + 1]), (u2.at[own + nx - 2], u2.at[own - 2])),
        "u2far": (0, (u2.at[own + 2], u2.at[own + nx + 2]), (u2.at[own + nx - 3], u2.at[own - 3])),
        "u2corner": (0, (corner_of.at[1, 0], corner.at[1, 1]), (corner_of.at[1, 1], corner.at[1, 0])),
        "coarse": (0, (coarse.at[pl.ds(4, 2)], coarse.at[pl.ds(4 + cx, 2)]),
                   (coarse.at[pl.ds(2 + cx, 2)], coarse.at[pl.ds(2, 2)])),
        "strip": (1, (pack.at[0], strip.at[1]), (pack.at[0], strip.at[0])),
        "strip_a": (1, (pack_a, strip_a.at[1]), (pack_a, strip_a.at[0])),
        "line": (1, (pack.at[pl.ds(1, 2)], strip.at[pl.ds(4, 2)]), (pack.at[pl.ds(1, 2)], strip.at[pl.ds(2, 2)])),
    }
    names = list(exchanges)

    def copies(name):
        axis, low, high = exchanges[name]
        at = names.index(name)
        return [
            (
                pltpu.make_async_remote_copy(
                    src_ref=pair[0], dst_ref=pair[1], send_sem=send_sem.at[at, i], recv_sem=recv_sem.at[at, i],
                    device_id=to[2 * axis + i], device_id_type=MESH,
                ),
                has[2 * axis + i],
                has[2 * axis + 1 - i],
            )
            for i, pair in enumerate((low, high))
        ]

    def start(name):
        for copy, goes, _ in copies(name):
            @pl.when(goes)
            def _():
                copy.start()

    def arrive(*which):
        for name in which:
            for copy, _, comes in copies(name):
                @pl.when(comes)
                def _():
                    copy.wait_recv()

    lane = lax.broadcasted_iota(jnp.int32, (levels, ny), 1)
    lane_c = lax.broadcasted_iota(jnp.int32, (levels, 128), 1)
    level = lax.broadcasted_iota(jnp.int32, (levels, ny), 0)
    inner = lane_c % 8 < 4
    row_c = lane_c // 8

    def packed(rows, base=None):
        result = jnp.zeros((levels, 128), f32) if base is None else base
        for e, value in rows:
            ends = jnp.where(lane_c < 4, value[:, :128], value[:, value.shape[1] - 128 :])
            result = jnp.where(row_c == e, pltpu.roll(ends, 8 * e + 4, 1), result)
        return result

    def strips(mine, low, high):
        return jnp.concatenate([jnp.where(inner, low, mine), jnp.where(inner, mine, high)], axis=1)

    def squeeze(tile, e):
        result = jnp.zeros((8, 128), f32)
        for b in range(levels // 8):
            part = pltpu.roll(tile[8 * b : 8 * b + 8], (16 * b - 8 * e) % 128, 1)
            result = jnp.where(lane_c[:8] // 16 == b, part, result)
        return result

    def unsqueeze(tile, e):
        return jnp.concatenate([pltpu.roll(tile, (8 * e - 16 * b) % 128, 1) for b in range(levels // 8)], axis=0)

    inputs[0].wait()
    for x in (0, 1, nx - 2, nx - 1) + tuple(range(2, nx - 2)):
        rhs_x[own + x] = jnp.concatenate(
            [rhs_ref[pl.ds(x + nx * t, levels, stride=tiles * nx), :] for t in range(tiles)], axis=1
        )
    peers = sum(h.astype(jnp.int32) for h in has)
    for s in strides[1:]:
        peers = peers + (w >= s).astype(jnp.int32) + (w < n_w - s).astype(jnp.int32)
    pl.semaphore_wait(barrier, peers)
    inputs[2].wait()
    start("areas")
    start("rhs")
    pack_rhs = packed([(e, rhs_x[e]) for e in range(own, own + nx)])
    pack[0] = pack_rhs
    start("strip")

    inputs[1].wait()
    zero, one = jnp.float32(0.0), jnp.float32(1.0)
    t_before, t_now, p_before, p_now = zero, one, zero, one
    for i in range(levels):
        j = levels - 1 - i
        here, there = stiff_ref[i], stiff_ref[j]
        theta[i : i + 1, :] = jnp.full((1, 128), t_now, f32)
        phi[j : j + 1, :] = jnp.full((1, 128), p_now, f32)
        stiff_b[i : i + 1, :] = jnp.full((1, 128), here, f32)
        t_before, t_now = t_now, (here * 0.125 + 1.0) * t_now - 0.0625 * t_before
        p_before, p_now = p_now, (there * 0.125 + 1.0) * p_now - 0.0625 * p_before
    whole = jnp.full((levels, 128), t_now, f32)
    row = lax.broadcasted_iota(jnp.int32, (levels, 128), 0)
    col = lax.broadcasted_iota(jnp.int32, (levels, 128), 1)
    apart = jnp.abs(row - col)
    decay = jnp.full((levels, 128), 0.4 * 0.125, f32)
    for b in range(6):
        decay = jnp.where((apart & (1 << b)) != 0, decay * (0.25 ** (1 << b)), decay)
    t_col, p_col = theta[...], phi[...]
    same = row == col
    t_row = jnp.sum(jnp.where(same, t_col, 0.0), axis=0, keepdims=True)
    p_row = jnp.sum(jnp.where(same, p_col, 0.0), axis=0, keepdims=True)
    inverse = (jnp.where(row <= col, t_col * p_row, p_col * t_row) * decay / whole)[:, :levels]
    inv_hi, inv_lo = halves(inverse)
    weights = jnp.concatenate([inv_hi, inv_hi, inv_lo], axis=1)

    def apply(value):
        high, low = halves(value)
        stacked = jnp.concatenate([high, low, high], axis=0)
        return jnp.dot(weights, stacked, preferred_element_type=f32)

    def area(e):
        return wide_a[nx + e - own : nx + e - own + 1, :]

    def sides(u, sides_of, e):
        n = u.shape[1]
        index = lane[:, :n]
        low = pltpu.roll(sides_of[:, :128], (125 - 8 * e) % 128, 1)
        high = pltpu.roll(sides_of[:, 128:], (123 - 8 * e) % 128, 1)
        if n == 128:
            down = jnp.where(index == 0, low, pltpu.roll(u, 1, 1))
            return down + jnp.where(index == n - 1, high, pltpu.roll(u, n - 1, 1))
        edge = jnp.concatenate([low, high], axis=1)
        down = jnp.where(index == 0, edge, pltpu.roll(u, 1, 1))
        return down + jnp.where(index == n - 1, edge, pltpu.roll(u, n - 1, 1))

    def smooth(field, sides_of, e):
        u = field[e]
        nb = field[e - 1] + field[e + 1] + sides(u, sides_of, e)
        a = area(e)
        return 0.6 * u + apply(rhs_x[e] + (4.0 - 4.0 * a) * u + a * nb)

    def smooth_strip(s, right_side, a):
        nb = pltpu.roll(s, 1, 1) + pltpu.roll(s, ny - 1, 1) + pltpu.roll(s, 8, 1) + pltpu.roll(s, ny - 8, 1)
        return 0.6 * s + apply(right_side + (4.0 - 4.0 * a) * s + a * nb)

    def horizontal(field, sides_of, e):
        u = field[e]
        nb = field[e - 1] + field[e + 1] + sides(u, sides_of, e)
        return u, rhs_x[e] - area(e) * (4.0 * u - nb)

    def vertical(v):
        above = jnp.where(level == levels - 1, 0.0, pltpu.roll(v, levels - 1, 0))
        below = jnp.where(level == 0, 0.0, pltpu.roll(v, 1, 0))
        s = jnp.concatenate([stiff_b[...]] * (ny // 128), axis=1)
        return (s + 4.0) * v - 2.0 * (above + below)

    pick = jnp.where(
        lax.broadcasted_iota(jnp.int32, (ny, cy), 0) // 2 == lax.broadcasted_iota(jnp.int32, (ny, cy), 1),
        1.0, 0.0,
    ).astype(bf16)
    spread = jnp.where(
        lax.broadcasted_iota(jnp.int32, (cy, ny), 1) // 2 == lax.broadcasted_iota(jnp.int32, (cy, ny), 0),
        1.0, 0.0,
    ).astype(bf16)
    fine_lane = lax.broadcasted_iota(jnp.int32, (128, 128), 1)
    spread_strip = jnp.where(
        lax.broadcasted_iota(jnp.int32, (128, 128), 0)
        == 8 * ((fine_lane // 8 + 3) // 2) + 2 + (fine_lane % 8) // 2,
        1.0, 0.0,
    ).astype(bf16)

    def exact(value, matrix):
        rows = value.shape[0]
        high, low = halves(value)
        both = jnp.dot(jnp.concatenate([high, low], axis=0), matrix, preferred_element_type=f32)
        return both[:rows] + both[rows:]

    for e in range(own, own + nx):
        u1[e] = apply(rhs_x[e])

    arrive("strip")
    halo = jnp.where(inner, strip[0], strip[1])
    corner_of[0, 0] = squeeze(halo, own)
    corner_of[0, 1] = squeeze(halo, own + nx - 2)
    start("corner")
    first = apply(strips(pack_rhs, halo, halo))
    for e in range(own + 1, own + nx - 1):
        u2[e] = smooth(u1, first, e)

    arrive("areas")
    eight = lane_c[:8]
    packed_a = jnp.zeros((8, 128), f32)
    for e in range(0, nx + 6):
        v = jnp.broadcast_to(area(e), (8, ny))
        v = pltpu.roll(jnp.where(eight < 4, v[:, :128], v[:, ny - 128 :]), 8 * e + 4, 1)
        packed_a = jnp.where(eight // 8 == e, v, packed_a)
    sums = []
    for x in range(-2, cx + 2):
        at = nx + 2 * x
        sums.append(jnp.broadcast_to(0.0625 * (wide_a[at : at + 1, :] + wide_a[at + 1 : at + 2, :]), (8, ny)))
    coef = exact(jnp.concatenate(sums, axis=0), pick)
    coef = {x: coef[8 * (x + 2) : 8 * (x + 2) + 8] for x in range(-2, cx + 2)}
    packed_c = jnp.zeros((8, 128), f32)
    for x in range(-2, cx + 2):
        v = pltpu.roll(coef[x], 8 * (x + 3) + 4, 1)
        packed_c = jnp.where(eight // 8 == x + 3, v, packed_c)
    pack_a[0:8, :] = packed_a
    pack_a[8:16, :] = packed_c
    start("strip_a")

    arrive("rhs")
    start("u2near")
    outer = (own - 2, own - 1, own + nx, own + nx + 1)
    for e in outer:
        u1[e] = apply(rhs_x[e])
    pack_all = packed([(e, rhs_x[e]) for e in outer], pack_rhs)
    arrive("corner", "strip_a")
    halo = jnp.where(
        row_c < own, unsqueeze(corner[0, 0], own - 2),
        jnp.where(row_c >= own + nx, unsqueeze(corner[0, 1], own + nx), halo),
    )
    rhs_strip = strips(pack_all, halo, halo)
    inner_a = eight % 8 < 4

    def strips_a(low, high, mine):
        return jnp.concatenate([jnp.where(inner_a, low, mine), jnp.where(inner_a, mine, high)], axis=1)[:1]

    a_strip = strips_a(strip_a[0, 0:8, :], strip_a[1, 0:8, :], packed_a)
    c_strip = strips_a(strip_a[0, 8:16, :], strip_a[1, 8:16, :], packed_c)
    first = apply(rhs_strip)
    for e in (own - 1, own, own + nx - 1, own + nx):
        u2[e] = smooth(u1, first, e)
    second = smooth_strip(first, rhs_strip, a_strip)

    s = stiff_b[...]
    keep = jnp.sqrt(s + 0.25 * s * s) - 0.5 * s
    r = 1.0 - keep
    power = [jnp.ones_like(r)]
    for _ in range(4 * cx + 6):
        power.append(power[-1] * r)
    is_last = w == n_w - 1
    far = jnp.ones_like(r)
    base = power[2 * cx]
    steps = jnp.maximum(n_w - 2 - w, 0)
    for b in range(len(strides)):
        far = jnp.where((steps >> b) % 2 == 1, far * base, far)
        base = base * base
    tail = jnp.where(is_last, power[0], far * power[2 * cx])
    scale = keep / (1.0 + r)

    for x in range(cx):
        e = own + 2 * x
        u_a, h_a = horizontal(u2, second, e)
        u_b, h_b = horizontal(u2, second, e + 1)
        coarse[4 + x] = exact(0.25 * (h_a + h_b - vertical(u_a + u_b)), pick)
    mine = [coarse[4 + x] for x in range(cx)]
    forward = mine[0]
    for x in range(1, cx):
        forward = mine[x] + r * forward
    backward = sum((power[x] - tail * power[2 * cx - x]) * mine[x] for x in range(cx))
    enter = jnp.zeros_like(forward)
    leave = jnp.zeros_like(forward)
    step_all = power[cx]
    step_less = None
    scans = []
    for i, s in enumerate(strides):
        scan_f[i] = forward
        scan_z[i] = backward
        right = pltpu.make_async_remote_copy(
            src_ref=scan_f.at[i], dst_ref=scan_rf.at[i], send_sem=scan_send.at[i, 0], recv_sem=scan_recv.at[i, 0],
            device_id={"wide": jnp.minimum(w + s, n_w - 1)}, device_id_type=MESH,
        )
        left = pltpu.make_async_remote_copy(
            src_ref=scan_z.at[i], dst_ref=scan_rz.at[i], send_sem=scan_send.at[i, 1], recv_sem=scan_recv.at[i, 1],
            device_id={"wide": jnp.maximum(w - s, 0)}, device_id_type=MESH,
        )
        scans.append((right, left, s))

        @pl.when(w < n_w - s)
        def _():
            right.start()

        @pl.when(w >= s)
        def _():
            left.start()

        if i == 0:
            start("coarse")
            start("u2far")
            halo = jnp.where(inner, second[:, :128], second[:, 128:])
            corner_of[1, 0] = squeeze(halo, own + 1)
            corner_of[1, 1] = squeeze(halo, own + nx - 3)
            start("u2corner")

        @pl.when(w >= s)
        def _():
            right.wait_recv()

        @pl.when(w < n_w - s)
        def _():
            left.wait_recv()

        got_f, got_z = scan_rf[i], scan_rz[i]
        forward = forward + step_all * got_f
        backward = backward + step_all * got_z
        enter = enter + (step_less * got_f if i else got_f)
        leave = leave + (step_less * got_z if i else got_z)
        step_less = step_less * step_all if i else step_all
        step_all = step_all * step_all

    arrive("coarse")
    inverse_r = 1.0 / r
    image = {
        t: 1.0 - jnp.where(is_last, power[max(2 * cx - 2 * t, 0)], far * power[4 * cx - 2 * t])
        for t in range(-3, cx + 3)
    }
    before = {-1: enter}
    for t in range(cx + 2):
        before[t] = coarse[4 + t] + r * before[t - 1]
    for t in (-2, -3):
        before[t] = (before[t + 1] - coarse[4 + t + 1]) * inverse_r
    after = {cx: leave}
    for t in reversed(range(-2, cx)):
        after[t] = image[t] * coarse[4 + t] + r * after[t + 1]
    for t in (cx + 1, cx + 2):
        after[t] = (after[t - 1] - image[t - 1] * coarse[4 + t - 1]) * inverse_r
    for t in range(-3, cx + 3):
        if t < cx:
            value = scale * (image[t] * before[t] + r * after[t + 1])
        else:
            value = scale * (image[t] * r * before[t - 1] + after[t])
        if t < 0:
            value = jnp.where(w == 0, 0.0, value)
        if t >= cx:
            value = jnp.where(is_last, 0.0, value)
        line[4 + t] = value
    pack_c = packed([(t + 3, coarse[4 + t]) for t in range(-2, cx + 2)])
    pack_l = packed([(t + 3, line[4 + t]) for t in range(-3, cx + 3)])
    pack[1] = pack_c
    pack[2] = pack_l
    start("line")

    arrive("u2near", "u2far", "u2corner")
    halo = jnp.where(
        row_c < own - 1, unsqueeze(corner[1, 0], own - 3),
        jnp.where(row_c > own + nx, unsqueeze(corner[1, 1], own + nx + 1), halo),
    )
    second = strips(packed([(e, u2[e]) for e in range(nx + 6)]), halo, halo)

    arrive("line")
    c_sides = strips(pack_c, strip[2], strip[4])
    l_sides = strips(pack_l, strip[3], strip[5])

    def correction(x):
        v = line[4 + x]
        nb = line[3 + x] + line[5 + x] + sides(v, l_sides, x + 3)
        a = coef[x][:1]
        return exact(0.6 * v + apply(coarse[4 + x] + (4.0 - 4.0 * a) * v + a * nb), spread)

    for x in range(-2, cx + 2):
        value = correction(x)
        for e in (own + 2 * x, own + 2 * x + 1):
            if 0 <= e < nx + 6:
                u3[e] = u2[e] + value
    fix = smooth_strip(l_sides, c_sides, c_strip)
    fix = exact(jnp.concatenate([fix[:, :128], fix[:, 128:]], axis=0), spread_strip)
    third = second + jnp.concatenate([fix[:levels], fix[levels:]], axis=1)
    for e in range(1, nx + 5):
        u4[e] = smooth(u3, third, e)
    fourth = smooth_strip(third, rhs_strip, a_strip)
    for e in range(2, nx + 4):
        p[e] = smooth(u4, fourth, e)
    fifth = smooth_strip(fourth, rhs_strip, a_strip)
    for x in range(nx):
        u, h = horizontal(p, fifth, own + x)
        left_over = h - vertical(u)
        for t in range(tiles):
            at = pl.ds(x + nx * t, levels, stride=tiles * nx)
            p_out[at, :] = u[:, 128 * t : 128 * t + 128]
            r_out[at, :] = left_over[:, 128 * t : 128 * t + 128]

    for name in names:
        for copy, goes, _ in copies(name):
            @pl.when(goes)
            def _():
                copy.wait_send()
    for right, left, s in scans:
        @pl.when(w < n_w - s)
        def _():
            right.wait_send()

        @pl.when(w >= s)
        def _():
            left.wait_send()


def local(n_w, n_n, rhs, areas, stiffness):
    levels, nx, ny = rhs.shape
    cx, tiles = nx // 2, ny // 128
    steps = max(1, (n_w - 1).bit_length())
    vmem = lambda *shape: pltpu.VMEM(shape, f32)
    whole = pl.BlockSpec(memory_space=pltpu.VMEM)
    outs = pl.pallas_call(
        functools.partial(kernel, n_w, n_n, nx, ny, levels),
        out_shape=[jax.ShapeDtypeStruct((levels * nx * tiles, 128), f32)] * 2,
        in_specs=[pl.BlockSpec(memory_space=pltpu.HBM)] * 3,
        out_specs=[whole, whole],
        scratch_shapes=[
            vmem(levels * nx * tiles, 128), pltpu.SMEM((levels,), f32), pltpu.SemaphoreType.DMA((3,)),
        ]
        + [vmem(nx + 6, levels, ny)] * 6
        + [
            vmem(3 * nx, ny), vmem(cx + 8, levels, 128), vmem(cx + 8, levels, 128),
            vmem(3, levels, 128), vmem(6, levels, 128), vmem(2, 2, 8, 128), vmem(2, 2, 8, 128),
            vmem(16, 128), vmem(2, 16, 128),
            vmem(steps, levels, 128), vmem(steps, levels, 128),
            vmem(steps, levels, 128), vmem(steps, levels, 128),
            vmem(levels, 128), vmem(levels, 128), vmem(levels, 128),
            pltpu.SemaphoreType.DMA((10, 2)), pltpu.SemaphoreType.DMA((10, 2)),
            pltpu.SemaphoreType.DMA((steps, 2)), pltpu.SemaphoreType.DMA((steps, 2)),
        ],
        compiler_params=pltpu.CompilerParams(
            collective_id=0, has_side_effects=True, vmem_limit_bytes=56 * 1024 * 1024
        ),
        cost_estimate=pl.CostEstimate(flops=80_000_000, bytes_accessed=1_600_000, transcendentals=0),
    )(rhs.reshape(levels, nx, tiles, 128).transpose(0, 2, 1, 3).reshape(-1, 128), areas, stiffness)
    return tuple(v.reshape(levels, tiles, nx, 128).transpose(0, 2, 1, 3).reshape(rhs.shape) for v in outs)


def solution(mesh):
    placed = (P(None, "wide", "narrow"), P("wide", "narrow"), P())
    return jax.shard_map(
        functools.partial(local, mesh.shape["wide"], mesh.shape["narrow"]),
        mesh=mesh,
        in_specs=placed,
        out_specs=(P(None, "wide", "narrow"), P(None, "wide", "narrow")),
        check_vma=False,
    )
```
